32 devices in a mesh: replica: 4 (over y, x), fsdp: 8 (over z, core).
Axes of the slice: x: 2, y: 2, z: 4, core: 2. Of those that a mesh axis runs over, the one named last changes fastest.
Arguments:
- tokens: bfloat16 [4, 3072, 4096], P('replica', 'fsdp'), may hold values from -16 to 16
- positions: int32 [4, 3072], P('replica', 'fsdp'), may hold values from 0 to 383, as said below
- partner: int32 [4], replicated, may hold values from 0 to 3, as said below
- weights: bfloat16 [4, 4096, 3072], P('replica', 'fsdp'), may hold values from -6 to 6
- anchor: float32 [4, 4096, 3072], P('replica', 'fsdp'), may hold values from -6 to 6
- momentum: float32 [4, 4096, 3072], P('replica', 'fsdp'), may hold values from -6 to 6
Outputs:
- context: bfloat16 [4, 3072, 2048], P('replica', 'fsdp')
- new_params: float32 [4, 4096, 3072], P('replica', 'fsdp')
- new_momentum: float32 [4, 4096, 3072], P('replica', 'fsdp')
The draws below stay inside these ranges and needn't reach their ends.
Inputs may be any that keep to these rules, and one draw needn't show every extreme that they name: partner pairs the replicas: partner[partner[r]] = r and partner[r] != r. positions count up by one from 0 within each document; every document lies within one aligned block of 384 tokens, and in each replica the first block is one document.
All inputs are finite; a program needn't handle non-finite values.
Results may differ from the reference program's by a relative error of at most 0.011.
Values may be sent and summed in bfloat16 or wider, within the bound.
No kernel may reach another device: no remote copies, remote signals or barrier semaphores. Data moves between devices by JAX's collectives and lax.ppermute only.
A program may use at most 128 MiB of HBM per device.

```python
import jax
import jax.numpy as jnp
from jax import lax

D = 4096
HEADS = 16
KV_HEADS = 4
HEAD_DIM = 128
TOK_DEV = 384
COLUMNS = 3072
REPLICAS = 4
TOKENS = 3072


def draw_tokens(key, part):
    key = jax.random.fold_in(key, 11)
    base = jax.random.normal(jax.random.fold_in(key, 1), (REPLICAS, TOKENS, D), jnp.float32)
    values = jnp.clip(base, -6.0, 6.0)
    return values.astype(jnp.bfloat16)


def draw_positions(key, part):
    key = jax.random.fold_in(key, 23)
    blocks = TOKENS // TOK_DEV
    ordinal = jnp.arange(TOK_DEV, dtype=jnp.int32)
    starts = jax.random.randint(key, (REPLICAS, blocks, TOK_DEV), 0, TOK_DEV) < 4
    starts = starts | (ordinal == 0)[None, None, :]
    single = (jnp.arange(blocks, dtype=jnp.int32) == 0)[None, :, None] & (ordinal > 0)[None, None, :]
    starts = starts & jnp.logical_not(single)
    latest = lax.cummax(jnp.where(starts, ordinal[None, None, :], 0), axis=2)
    return (ordinal[None, None, :] - latest).reshape(REPLICAS, TOKENS).astype(jnp.int32)


def draw_partner(key, part):
    key = jax.random.fold_in(key, 37)
    order = jax.random.permutation(key, REPLICAS).astype(jnp.int32)
    mates = order.reshape(REPLICAS // 2, 2)[:, ::-1].reshape(REPLICAS)
    return jnp.zeros((REPLICAS,), jnp.int32).at[order].set(mates)


def shard_levels(rng, extent, shards, least, largest):
    level = 1.0
    for axis_at, parts in shards:
        heights = jax.random.uniform(jax.random.fold_in(jax.random.fold_in(rng, 6), axis_at), (parts,), jnp.float32, least / len(shards), largest / len(shards))
        level = level * jnp.repeat(jnp.exp(heights), extent[axis_at] // parts).reshape((-1,) + (1,) * (len(extent) - 1 - axis_at))
    return level


def centred(own_key, extent, scale, reach, cuts=(), held_as=jnp.bfloat16):
    loudness = shard_levels(own_key, extent, cuts, -0.22, 0.18) if cuts else 1.0
    entries = jax.random.normal(own_key, extent, jnp.float32) * scale * loudness
    return jnp.minimum(jnp.maximum(entries, -reach), reach).astype(held_as)


def setup_inputs(seed: int = 0) -> dict:
    key_list = jax.random.split(jax.random.key(seed), 7)
    tokens = draw_tokens(jax.random.fold_in(key_list[6], 71), 0)
    positions = draw_positions(jax.random.fold_in(key_list[6], 71), 0)
    partner = draw_partner(jax.random.fold_in(key_list[6], 71), 0)
    weights = centred(key_list[3], (REPLICAS, D, COLUMNS), 1.0, 6.0, ((0, 4), (1, 8)))
    anchor = centred(key_list[4], (REPLICAS, D, COLUMNS), 1.0, 6.0, ((0, 4), (1, 8)), jnp.float32)
    momentum = centred(key_list[5], (REPLICAS, D, COLUMNS), 1.0, 6.0, ((0, 4), (1, 8)), jnp.float32)
    return {"tokens": tokens, "positions": positions, "partner": partner, "weights": weights, "anchor": anchor, "momentum": momentum}


ROPE_BASE = 500000.0
MOMENTUM_RATE = 0.9
OUTER_RATE = 0.7


def rotate(heads, places):
    half = heads.shape[-1] // 2
    frequency = ROPE_BASE ** (-(jnp.arange(half, dtype=jnp.float32) * 2.0) / heads.shape[-1])
    angles = places.astype(jnp.float32)[:, None] * frequency[None, :]
    cosine = jnp.cos(angles)[:, None, :]
    sine = jnp.sin(angles)[:, None, :]
    first = heads[..., :half]
    second = heads[..., half:]
    return jnp.concatenate([first * cosine - second * sine, second * cosine + first * sine], -1)


def attend(projected, places):
    count = projected.shape[0]
    width_q = HEADS * HEAD_DIM
    width_kv = KV_HEADS * HEAD_DIM
    group = HEADS // KV_HEADS
    scaled = projected * (D ** -0.5)
    query = rotate(scaled[:, :width_q].reshape(count, HEADS, HEAD_DIM), places).astype(jnp.bfloat16)
    keys = rotate(scaled[:, width_q:width_q + width_kv].reshape(count, KV_HEADS, HEAD_DIM), places).astype(jnp.bfloat16)
    values = scaled[:, width_q + width_kv:].reshape(count, KV_HEADS, HEAD_DIM).astype(jnp.bfloat16)
    query = query.reshape(count, KV_HEADS, group, HEAD_DIM)
    ordinal = jnp.arange(count, dtype=jnp.int32)
    distance = ordinal[:, None] - ordinal[None, :]
    visible = (distance >= 0) & (distance <= places[:, None])
    scores = jnp.einsum("tkge,ske->kgts", query.astype(jnp.float32), keys.astype(jnp.float32)) * (HEAD_DIM ** -0.5)
    scores = jnp.where(visible[None, None], scores, -1e30)
    highest = jnp.max(scores, -1, keepdims=True)
    exponent = jnp.exp(scores - highest)
    probabilities = (exponent / jnp.sum(exponent, -1, keepdims=True)).astype(jnp.bfloat16)
    context = jnp.einsum("kgts,ske->tkge", probabilities.astype(jnp.float32), values.astype(jnp.float32))
    return context.reshape(count, width_q).astype(jnp.bfloat16)


def reference(tokens, positions, partner, weights, anchor, momentum):
    def one_replica(items):
        rep_tokens, rep_places, rep_weights = items

        def one_device(block):
            rows, places = block
            projected = jnp.dot(rows, rep_weights, preferred_element_type=jnp.float32)
            return attend(projected, places)

        blocks = lax.map(one_device, (rep_tokens.reshape(-1, TOK_DEV, D), rep_places.reshape(-1, TOK_DEV)))
        return blocks.reshape(TOKENS, HEADS * HEAD_DIM)

    context = lax.map(one_replica, (tokens, positions, weights))
    pseudo = anchor - weights.astype(jnp.float32)
    grad_mean = 0.5 * (pseudo + jnp.take(pseudo, partner, axis=0))
    mom_mean = 0.5 * (momentum + jnp.take(momentum, partner, axis=0))
    new_momentum = MOMENTUM_RATE * mom_mean + grad_mean
    new_params = anchor - OUTER_RATE * (grad_mean + MOMENTUM_RATE * new_momentum)
    return (context, new_params, new_momentum)
```

```python
import jax
import jax.numpy as jnp
from jax import lax
from jax.sharding import PartitionSpec as P

D = 4096
HEADS = 16
KV_HEADS = 4
HEAD_DIM = 128


ROPE_BASE = 500000.0
MOMENTUM_RATE = 0.9
OUTER_RATE = 0.7


def rotate(heads, places):
    half = heads.shape[-1] // 2
    frequency = ROPE_BASE ** (-(jnp.arange(half, dtype=jnp.float32) * 2.0) / heads.shape[-1])
    angles = places.astype(jnp.float32)[:, None] * frequency[None, :]
    cosine = jnp.cos(angles)[:, None, :]
    sine = jnp.sin(angles)[:, None, :]
    first = heads[..., :half]
    second = heads[..., half:]
    return jnp.concatenate([first * cosine - second * sine, second * cosine + first * sine], -1)


def attend(projected, places):
    count = projected.shape[0]
    width_q = HEADS * HEAD_DIM
    width_kv = KV_HEADS * HEAD_DIM
    group = HEADS // KV_HEADS
    scaled = projected * D ** (-0.5)
    query = rotate(scaled[:, :width_q].reshape(count, HEADS, HEAD_DIM), places).astype(jnp.bfloat16)
    keys = rotate(
        scaled[:, width_q : width_q + width_kv].reshape(count, KV_HEADS, HEAD_DIM), places
    ).astype(jnp.bfloat16)
    values = scaled[:, width_q + width_kv :].reshape(count, KV_HEADS, HEAD_DIM).astype(jnp.bfloat16)
    query = query.reshape(count, KV_HEADS, group, HEAD_DIM)
    ordinal = jnp.arange(count, dtype=jnp.int32)
    distance = ordinal[:, None] - ordinal[None, :]
    visible = (distance >= 0) & (distance <= places[:, None])
    scores = jnp.einsum(
        "tkge,ske->kgts", query, keys, preferred_element_type=jnp.float32
    ) * HEAD_DIM ** (-0.5)
    scores = jnp.where(visible[None, None], scores, -1e30)
    highest = jnp.max(scores, -1, keepdims=True)
    exponent = jnp.exp(scores - highest)
    probabilities = (exponent / jnp.sum(exponent, -1, keepdims=True)).astype(jnp.bfloat16)
    context = jnp.einsum(
        "kgts,ske->tkge", probabilities, values, preferred_element_type=jnp.float32
    )
    return context.reshape(count, width_q).astype(jnp.bfloat16)


def pairings(count):
    if count == 0:
        return [{}]
    found = []

    def extend(left, pairs):
        if not left:
            found.append(dict(pairs))
            return
        first = left[0]
        for mate in left[1:]:
            rest = [r for r in left if r not in (first, mate)]
            extend(rest, pairs + [(first, mate), (mate, first)])

    extend(list(range(count)), [])
    return found


def send_to_mate(values, pairs):
    return [lax.ppermute(value, "replica", sorted(pairs.items())) for value in values]


def exchange_any(values, partner, count):
    me = lax.axis_index("replica")
    received = [jnp.zeros_like(value) for value in values]
    order = jnp.arange(count, dtype=jnp.int32)
    for step in range(1, count):
        perm = [(r, (r + step) % count) for r in range(count)]

        def one_round(held):
            came = [lax.ppermute(value, "replica", perm) for value in values]
            mine = partner[me] == (me + count - step) % count
            return [jnp.where(mine, new, old) for new, old in zip(came, held)]

        used = jnp.any(partner == (order + step) % count)
        received = lax.cond(used, one_round, lambda held: held, received)
    return received


def outer_step(exchange, weights, anchor, momentum):
    pseudo = anchor[0] - weights[0].astype(jnp.float32)
    mate_pseudo, mate_momentum = exchange(
        [pseudo.astype(jnp.bfloat16), momentum[0].astype(jnp.bfloat16)]
    )
    grad_mean = 0.5 * (pseudo + mate_pseudo.astype(jnp.float32))
    mom_mean = 0.5 * (momentum[0] + mate_momentum.astype(jnp.float32))
    new_momentum = MOMENTUM_RATE * mom_mean + grad_mean
    new_params = anchor[0] - OUTER_RATE * (grad_mean + MOMENTUM_RATE * new_momentum)
    return (new_params[None], new_momentum[None])


def attention_step(tokens, positions, weights):
    rows = tokens[0]
    places = positions[0]
    projected = jnp.dot(
        rows,
        lax.all_gather(weights, "fsdp", axis=1, tiled=True)[0],
        preferred_element_type=jnp.float32,
    )
    return attend(projected, places)[None]


def step(exchange, tokens, positions, weights, anchor, momentum):
    context = attention_step(tokens, positions, weights)
    new_params, new_momentum = outer_step(exchange, weights, anchor, momentum)
    return (context, new_params, new_momentum)


def body(tokens, positions, partner, weights, anchor, momentum):
    count = lax.axis_size("replica")
    arrays = (tokens, positions, weights, anchor, momentum)
    if count > 4:
        return step(lambda values: exchange_any(values, partner, count), *arrays)
    branches = [
        lambda *held, pairs=pairs: step(lambda values: send_to_mate(values, pairs), *held)
        for pairs in pairings(count)
    ]
    return lax.switch(partner[0] - 1, branches, *arrays)


def solution(mesh):
    placed = (
        P("replica", "fsdp", None),
        P("replica", "fsdp"),
        P(),
        P("replica", "fsdp", None),
        P("replica", "fsdp", None),
        P("replica", "fsdp", None),
    )
    return jax.shard_map(
        body,
        mesh=mesh,
        in_specs=placed,
        out_specs=(
            P("replica", "fsdp", None),
            P("replica", "fsdp", None),
            P("replica", "fsdp", None),
        ),
        check_vma=False,
    )
```

```python
import jax
import jax.numpy as jnp
from jax import lax
from jax.experimental import pallas as pl
from jax.experimental.pallas import tpu as pltpu
from jax.sharding import PartitionSpec as P

D = 4096
HEADS = 16
KV_HEADS = 4
HEAD_DIM = 128


ROPE_BASE = 500000.0
MOMENTUM_RATE = 0.9
OUTER_RATE = 0.7


def rotate(heads, places):
    half = heads.shape[-1] // 2
    frequency = ROPE_BASE ** (-(jnp.arange(half, dtype=jnp.float32) * 2.0) / heads.shape[-1])
    angles = places.astype(jnp.float32)[:, None] * frequency[None, :]
    cosine = jnp.cos(angles)[:, None, :]
    sine = jnp.sin(angles)[:, None, :]
    first = heads[..., :half]
    second = heads[..., half:]
    return jnp.concatenate([first * cosine - second * sine, second * cosine + first * sine], -1)


def attend(projected, places):
    count = projected.shape[0]
    width_q = HEADS * HEAD_DIM
    width_kv = KV_HEADS * HEAD_DIM
    group = HEADS // KV_HEADS
    scaled = projected * D ** (-0.5)
    query = rotate(scaled[:, :width_q].reshape(count, HEADS, HEAD_DIM), places).astype(jnp.bfloat16)
    keys = rotate(
        scaled[:, width_q : width_q + width_kv].reshape(count, KV_HEADS, HEAD_DIM), places
    ).astype(jnp.bfloat16)
    values = scaled[:, width_q + width_kv :].reshape(count, KV_HEADS, HEAD_DIM).astype(jnp.bfloat16)
    query = query.reshape(count, KV_HEADS, group, HEAD_DIM)
    ordinal = jnp.arange(count, dtype=jnp.int32)
    distance = ordinal[:, None] - ordinal[None, :]
    visible = (distance >= 0) & (distance <= places[:, None])
    scores = jnp.einsum(
        "tkge,ske->kgts", query, keys, preferred_element_type=jnp.float32
    ) * HEAD_DIM ** (-0.5)
    scores = jnp.where(visible[None, None], scores, -1e30)
    highest = jnp.max(scores, -1, keepdims=True)
    exponent = jnp.exp(scores - highest)
    probabilities = (exponent / jnp.sum(exponent, -1, keepdims=True)).astype(jnp.bfloat16)
    context = jnp.einsum(
        "kgts,ske->tkge", probabilities, values, preferred_element_type=jnp.float32
    )
    return context.reshape(count, width_q).astype(jnp.bfloat16)


def exchange_any(values, partner, count):
    me = lax.axis_index("replica")
    received = [jnp.zeros_like(value) for value in values]
    order = jnp.arange(count, dtype=jnp.int32)
    for step in range(1, count):
        perm = [(r, (r + step) % count) for r in range(count)]

        def one_round(held):
            came = [lax.ppermute(value, "replica", perm) for value in values]
            mine = partner[me] == (me + count - step) % count
            return [jnp.where(mine, new, old) for new, old in zip(came, held)]

        used = jnp.any(partner == (order + step) % count)
        received = lax.cond(used, one_round, lambda held: held, received)
    return received


def outer_step(exchange, weights, anchor, momentum):
    pseudo = anchor[0] - weights[0].astype(jnp.float32)
    mate_pseudo, mate_momentum = exchange(
        [pseudo.astype(jnp.bfloat16), momentum[0].astype(jnp.bfloat16)]
    )
    grad_mean = 0.5 * (pseudo + mate_pseudo.astype(jnp.float32))
    mom_mean = 0.5 * (momentum[0] + mate_momentum.astype(jnp.float32))
    new_momentum = MOMENTUM_RATE * mom_mean + grad_mean
    new_params = anchor[0] - OUTER_RATE * (grad_mean + MOMENTUM_RATE * new_momentum)
    return (new_params[None], new_momentum[None])


def attention_step(tokens, positions, weights):
    rows = tokens[0]
    places = positions[0]
    projected = jnp.dot(
        rows,
        lax.all_gather(weights, "fsdp", axis=1, tiled=True)[0],
        preferred_element_type=jnp.float32,
    )
    return attend(projected, places)[None]


LINE = 4
CORES = 2
SQUARE = 4
UNIT = HEAD_DIM
GROUP = HEADS // KV_HEADS
HALF_GROUPS = KV_HEADS // CORES
CHUNKS = (("k0", "k1", "v0", "v1"), ("q0",) * GROUP, ("q1",) * 2, ("q1",) * 2)
FIRST_UNIT = tuple(sum(len(c) for c in CHUNKS[:j]) for j in range(len(CHUNKS)))
HALF_UNITS = sum(len(c) for c in CHUNKS)
PAIR = 2 * UNIT
MIB = 1024 * 1024
SMALL = pl.CostEstimate(flops=1, bytes_accessed=1, transcendentals=0)
HBM = pl.BlockSpec(memory_space=pltpu.HBM)
MARK = jax.ShapeDtypeStruct((8, 128), jnp.float32)


def pairs_of_half(half):
    per_half = HEADS // CORES // 2
    pairs = [HEADS // 2 + half, (HEADS + KV_HEADS) // 2 + half]
    pairs += [half * per_half + at for at in range(per_half)]
    return jnp.stack([jnp.asarray(pair, jnp.int32) for pair in pairs])


def mark_spec():
    return pl.BlockSpec(MARK.shape, lambda *at: (0, 0))


def hand_kernel(lead, tokens, *refs):
    out, mark = refs[-2:]
    out[...] = tokens[...]
    mark[...] = jnp.zeros_like(mark)


def hand_tokens(tokens, lead):
    rows, columns = tokens.shape
    block = columns // LINE
    return pl.pallas_call(
        hand_kernel,
        grid_spec=pltpu.PrefetchScalarGridSpec(
            num_scalar_prefetch=1,
            grid=(LINE - 1,),
            in_specs=[pl.BlockSpec((rows, block), lambda at, lead: (0, lead[0] + at))],
            out_specs=(pl.BlockSpec((rows, block), lambda at, lead: (0, at)), mark_spec()),
        ),
        out_shape=(jax.ShapeDtypeStruct((rows, columns - block), tokens.dtype), MARK),
        compiler_params=pltpu.CompilerParams(vmem_limit_bytes=50 * MIB),
        cost_estimate=SMALL,
        name="hand_tokens",
    )(lead, tokens)


def pack_kernel(pairs, own, sibling, *refs):
    out, mark = refs[-2:]
    out[0] = own[...]
    out[1] = sibling[...]
    mark[...] = jnp.zeros_like(mark)


def pack(first, count, own, sibling, pairs, after=()):
    depth = own.shape[0]
    column = pl.BlockSpec((depth, PAIR), lambda at, pairs: (0, pairs[first + at]))
    return pl.pallas_call(
        pack_kernel,
        grid_spec=pltpu.PrefetchScalarGridSpec(
            num_scalar_prefetch=1,
            grid=(count,),
            in_specs=[column, column] + [HBM] * len(after),
            out_specs=(
                pl.BlockSpec((CORES, depth, PAIR), lambda at, pairs: (0, 0, at)),
                mark_spec(),
            ),
        ),
        out_shape=(jax.ShapeDtypeStruct((CORES, depth, count * PAIR), own.dtype), MARK),
        compiler_params=pltpu.CompilerParams(vmem_limit_bytes=50 * MIB),
        cost_estimate=SMALL,
        name="pack",
    )(pairs, own, sibling, *after)


def touch(value, *after):
    def kernel(*refs):
        refs[-1][...] = jnp.zeros_like(refs[-1])

    return pl.pallas_call(
        kernel,
        in_specs=[HBM] * (1 + len(after)),
        out_specs=(HBM, pl.BlockSpec(memory_space=pltpu.VMEM)),
        out_shape=(jax.ShapeDtypeStruct(value.shape, value.dtype), MARK),
        input_output_aliases={0: 0},
        cost_estimate=SMALL,
        name="touch",
    )(value, *after)


def project_kernel(groups, based, needs_middle, table, *refs):
    tokens, refs = refs[: 2 * groups], refs[2 * groups :]
    blocks, refs = refs[:groups], refs[groups:]
    out, mark = refs[-2:]
    mark[...] = jnp.zeros_like(mark)
    rows = tokens[0].shape[0]
    depth, span = blocks[0].shape[1:]
    tile = min(span, 512)
    core = table[0]

    def multiply():
        for half in range(CORES):
            here = slice(half * rows, (half + 1) * rows)
            for left in range(0, span, tile):
                columns = slice(left, left + tile)
                total = refs[0][here, columns] if based else None
                for group in range(groups):
                    source = tokens[2 * group + half]
                    for k in range(CORES):
                        taken = (core + k) % CORES * depth
                        taken = pl.ds(pl.multiple_of(taken, depth), depth)
                        part = jnp.dot(
                            source[:, taken],
                            blocks[group][k, :, columns],
                            preferred_element_type=jnp.float32,
                        )
                        total = part if total is None else total + part
                out[here, columns] = total.astype(out.dtype)

    if not needs_middle:
        multiply()
        return
    pl.when(table[1] == 1)(multiply)

    @pl.when(table[1] == 0)
    def _():
        out[...] = refs[0][...].astype(out.dtype) if based else jnp.zeros_like(out)


def project(span, table, groups, dtype, base=None, needs_middle=True, after=()):
    first_unit, width = span
    rows = groups[0][0][0].shape[0]
    depth = groups[0][2].shape[1]
    size = (CORES * rows, width * UNIT)
    token_specs, block_specs, arrays, blocks = [], [], [], []
    for tokens, slot, held, place in groups:
        token_specs += [
            pl.BlockSpec((rows, CORES * depth), lambda i, table, slot=slot: (0, table[slot]))
        ] * 2
        block_specs.append(
            pl.BlockSpec((CORES, depth, width * UNIT), lambda i, table, place=place: (0, 0, place))
        )
        arrays += list(tokens)
        blocks.append(held)
    bases = () if base is None else (base,)
    return pl.pallas_call(
        lambda *refs: project_kernel(len(groups), base is not None, needs_middle, *refs),
        grid_spec=pltpu.PrefetchScalarGridSpec(
            num_scalar_prefetch=1,
            grid=(1,),
            in_specs=token_specs
            + block_specs
            + [pl.BlockSpec(size, lambda i, table: (0, first_unit // width))] * len(bases)
            + [HBM] * len(after),
            out_specs=(pl.BlockSpec(size, lambda i, table: (0, 0)), mark_spec()),
        ),
        out_shape=(jax.ShapeDtypeStruct(size, dtype), MARK),
        compiler_params=pltpu.CompilerParams(vmem_limit_bytes=56 * MIB),
        cost_estimate=SMALL,
        name="project",
    )(table, *arrays, *blocks, *bases, *after)


def joined_rows(own, came, rows, unit):
    columns = slice(unit * UNIT, (unit + 1) * UNIT)
    return (own[rows, columns] + came[rows, columns].astype(jnp.float32)) * D ** (-0.5)


def turned(value, cosine, sine):
    return (value * cosine + pltpu.roll(value, HEAD_DIM // 2, 1) * sine).astype(jnp.bfloat16)


def keep_kernel(own, came, cosine, sine, *refs):
    keys, values, mark = refs[-3:]
    mark[...] = jnp.zeros_like(mark)
    count = cosine.shape[1]
    for block in range(CORES):
        rows = slice(block * count, (block + 1) * count)
        for group in range(HALF_GROUPS):
            key = joined_rows(own, came, rows, group)
            keys[group, block] = turned(key, cosine[block], sine[block])
            value = joined_rows(own, came, rows, HALF_GROUPS + group)
            values[group, block] = value.astype(jnp.bfloat16)


def keep_keys(own, came, cosine, sine, after=()):
    kept = jax.ShapeDtypeStruct((HALF_GROUPS, CORES) + cosine.shape[1:], jnp.bfloat16)
    whole = pl.BlockSpec(memory_space=pltpu.VMEM)
    return pl.pallas_call(
        keep_kernel,
        in_specs=[whole] * 4 + [HBM] * len(after),
        out_shape=(kept, kept, MARK),
        compiler_params=pltpu.CompilerParams(vmem_limit_bytes=24 * MIB),
        cost_estimate=SMALL,
        name="keep_keys",
    )(own, came, cosine, sine, *after)


def attend_kernel(heads, group, own, came, cosine, sine, places, keys, values, *refs):
    outs, mark, hidden = refs[-4:-2], refs[-2], refs[-1]
    mark[...] = jnp.zeros_like(mark)
    count = cosine.shape[1]
    tile = HEAD_DIM
    for block in reversed(range(CORES)):
        row = lax.broadcasted_iota(jnp.int32, (count, count), 0)
        distance = row - lax.broadcasted_iota(jnp.int32, (count, count), 1)
        visible = (distance >= 0) & (distance <= places[block])
        hidden[...] = jnp.where(visible, 0.0, -1e30)
        for head in range(heads):
            rows = slice(block * count, (block + 1) * count)
            query = turned(joined_rows(own, came, rows, head), cosine[block], sine[block])
            for top in range(0, count, tile):
                width = top + tile
                scores = lax.dot_general(
                    query[top:width],
                    keys[group, block, :width],
                    (((1,), (1,)), ((), ())),
                    preferred_element_type=jnp.float32,
                )
                scores = scores + hidden[top:width, :width]
                scores = (scores - jnp.max(scores, -1, keepdims=True)) * HEAD_DIM ** (-0.5)
                exponent = jnp.exp(scores)
                share = jnp.sum(exponent, -1, keepdims=True)
                mixed = jnp.dot(
                    exponent.astype(jnp.bfloat16),
                    values[group, block, :width],
                    preferred_element_type=jnp.float32,
                )
                outs[block][top:width, head * UNIT : (head + 1) * UNIT] = (mixed / share).astype(
                    jnp.bfloat16
                )


def attend_chunk(chunk, own, came, cosine, sine, places, held, after=()):
    count = cosine.shape[1]
    heads, group = len(CHUNKS[chunk]), int(CHUNKS[chunk][0][1])
    out = jax.ShapeDtypeStruct((count, heads * UNIT), jnp.bfloat16)
    whole = pl.BlockSpec(memory_space=pltpu.VMEM)
    return pl.pallas_call(
        lambda *refs: attend_kernel(heads, group, *refs),
        in_specs=[whole] * 7 + [HBM] * len(after),
        out_shape=(out, out, MARK),
        scratch_shapes=[pltpu.VMEM((count, count), jnp.float32)],
        compiler_params=pltpu.CompilerParams(vmem_limit_bytes=24 * MIB),
        cost_estimate=SMALL,
        name="attend_chunk",
    )(own, came, cosine, sine, places, *held, *after)


PARTS = 2
TILE = 64


def sent_kernel(lead, anchor, weights, momentum, *refs):
    out, mark = refs[-2:]
    mark[...] = jnp.zeros_like(mark)
    out[0] = momentum[...].astype(out.dtype)
    out[1] = (anchor[...] - weights[...].astype(jnp.float32)).astype(out.dtype)


def sent_part(part, anchor, weights, momentum, after=()):
    rows, columns = anchor.shape
    steps = rows // PARTS // TILE
    here = pl.BlockSpec((TILE, columns), lambda i, lead: (lead[0] * steps + i, 0))
    return pl.pallas_call(
        sent_kernel,
        grid_spec=pltpu.PrefetchScalarGridSpec(
            num_scalar_prefetch=1,
            grid=(steps,),
            in_specs=[here] * 3 + [HBM] * len(after),
            out_specs=(pl.BlockSpec((2, TILE, columns), lambda i, lead: (0, i, 0)), mark_spec()),
        ),
        out_shape=(
            jax.ShapeDtypeStruct((2, rows // PARTS, columns), jnp.bfloat16),
            MARK,
        ),
        compiler_params=pltpu.CompilerParams(vmem_limit_bytes=56 * MIB),
        cost_estimate=SMALL,
        name="sent_part",
    )(part, anchor, weights, momentum, *after)


def outer_kernel(steps, table, anchor, weights, momentum, *refs):
    new_params, new_momentum, mark = refs[-3:]
    mark[...] = jnp.zeros_like(mark)
    part = pl.program_id(0) // steps
    for at in range(4):

        @pl.when(table[part] == at)
        def _():
            mate = refs[at]
            start = anchor[...]
            pseudo = start - weights[...].astype(jnp.float32)
            grad_mean = 0.5 * (pseudo + mate[1].astype(jnp.float32))
            mom_mean = 0.5 * (momentum[...] + mate[0].astype(jnp.float32))
            moved = MOMENTUM_RATE * mom_mean + grad_mean
            new_momentum[...] = moved
            new_params[...] = start - OUTER_RATE * (grad_mean + MOMENTUM_RATE * moved)


def outer_update(table, anchor, weights, momentum, came, after=()):
    rows, columns = anchor.shape
    steps = rows // PARTS // TILE
    here = pl.BlockSpec((TILE, columns), lambda i, table: (i, 0))

    def chosen(at):
        return pl.BlockSpec(
            (2, TILE, columns),
            lambda i, table: (0, jnp.where(table[i // steps] == at, i % steps, 0), 0),
        )

    full = jax.ShapeDtypeStruct((rows, columns), jnp.float32)
    return pl.pallas_call(
        lambda *refs: outer_kernel(steps, *refs),
        grid_spec=pltpu.PrefetchScalarGridSpec(
            num_scalar_prefetch=1,
            grid=(PARTS * steps,),
            in_specs=[here] * 3 + [chosen(at) for at in range(4)] + [HBM] * len(after),
            out_specs=(here, here, pl.BlockSpec(MARK.shape, lambda i, table: (0, 0))),
        ),
        out_shape=(full, full, MARK),
        compiler_params=pltpu.CompilerParams(vmem_limit_bytes=56 * MIB),
        cost_estimate=SMALL,
        name="outer_update",
    )(table, anchor, weights, momentum, *came, *after)


def line_step(partner, tokens, positions, weights, anchor, momentum):
    rows, places = tokens[0], positions[0]
    own_rows = weights[0]
    start, moved = anchor[0], momentum[0]
    count, depth = rows.shape[0], own_rows.shape[0]
    me = lax.axis_index("fsdp")
    chip, core = me // CORES, me % CORES
    last = LINE - 1
    chunks = len(CHUNKS)

    def over(value, pairs):
        return lax.ppermute(value, "fsdp", pairs)

    cores = range(CORES)
    swap = [(f, f ^ 1) for f in range(LINE * CORES)]
    inward = [(a * CORES + c, b * CORES + c) for a, b in ((0, 1), (last, last - 1)) for c in cores]
    across = [(a * CORES + c, b * CORES + c) for a, b in ((1, 2), (2, 1)) for c in cores]
    outward = [(b, a) for a, b in inward]
    across += [(a * CORES + c, a * CORES + 1 - c) for a in (0, last) for c in cores]

    other_rows = over(own_rows, across)
    sibling_rows = over(own_rows, swap)
    lead = (chip < LINE // 2).astype(jnp.int32)
    handed, mark = hand_tokens(rows, lead[None])
    handed = over(handed, inward)

    distance = partner[0]
    part_rows = depth // PARTS

    along = [[(r, r ^ 1) for r in range(SQUARE)], [(r, r ^ 2) for r in range(SQUARE)]]
    values = (start, own_rows, moved)
    swapped = (distance == 2).astype(jnp.int32)
    first = []
    for part in (swapped, 1 - swapped):
        made, mark = sent_part(part[None], *values, (mark,))
        first.append(made)
    came = [lax.ppermute(first[at], "replica", along[at]) for at in range(2)]
    table = jnp.stack([jnp.where(distance == 3, 3, distance - 1), jnp.where(distance == 2, 3, 2)])

    pairs = pairs_of_half(core)
    packed, marks = [], (mark,)
    for j in range(chunks):
        made, mark = pack(
            FIRST_UNIT[j] // 2, len(CHUNKS[j]) // 2, own_rows, sibling_rows, pairs, marks
        )
        packed.append(made)
        marks = (mark,)
    sibling_tokens = over(rows, swap)
    both = jnp.stack([places, over(places, swap)])
    frequency = ROPE_BASE ** (
        -(jnp.arange(HEAD_DIM // 2, dtype=jnp.float32) * 2.0) / HEAD_DIM
    )
    angles = both.astype(jnp.float32)[:, :, None] * frequency
    cosine, sine = jnp.cos(angles), jnp.sin(angles)
    cosine = jnp.concatenate([cosine, cosine], -1)
    sine = jnp.concatenate([-sine, sine], -1)
    reach = both[:, :, None]

    near_chip = jnp.where(chip < LINE // 2, 0, last)
    middle = (chip > 0) & (chip < last)
    chips = jnp.stack([chip, last - chip, last - near_chip, near_chip])
    handed_chips = jnp.clip(chips - lead, 0, LINE - 2)
    spots = jnp.concatenate([jnp.stack([core, middle.astype(jnp.int32)]), chips, handed_chips])
    OWN, OTHER, FAR, NEAR, HANDED = 2, 3, 4, 5, 4
    every = (0, HALF_UNITS)
    ours = (rows, sibling_tokens)

    all_own, mark = pack(0, HALF_UNITS // 2, own_rows, sibling_rows, pairs, marks)
    own_sum, mark = project(
        every, spots, [(ours, OWN, all_own, 0)], jnp.float32, needs_middle=False,
        after=(mark, cosine, sine),
    )
    handed, mark = touch(handed, mark)
    theirs = (handed, over(handed, swap))
    near, far = [over(packed[0], inward)], []

    def stage(j, *after):
        near[j], mark = touch(near[j], *far[j - 1 :], *after)
        far.append(over(near[j], across))
        if j + 1 < chunks:
            near.append(over(touch(packed[j + 1], mark)[0], inward))
        return mark

    other_rows, mark = touch(other_rows, mark, near[0])
    mark = stage(0, mark)
    other_sibling_rows = over(other_rows, swap)
    came = [touch(value, mark)[0] for value in came]
    second = [jnp.where(distance == 3, came[1 - at], first[1 - at]) for at in range(2)]
    came += [lax.ppermute(second[at], "replica", along[at]) for at in range(2)]
    handed_sum, mark = project(
        every, spots, [(theirs, OWN + HANDED, all_own, 0)], jnp.float32, after=(mark, *second)
    )
    all_other, mark = pack(0, HALF_UNITS // 2, other_rows, other_sibling_rows, pairs, (mark,))
    handed_sum, mark = project(
        every, spots, [(theirs, OTHER + HANDED, all_other, 0)], jnp.float32, handed_sum,
        after=(mark,),
    )
    mark = stage(1, mark)
    own_sum, mark = project(
        every, spots, [(ours, OTHER, all_other, 0)], jnp.float32, own_sum, after=(mark,)
    )

    contexts, owns, backs = [], [], []

    def product(j, *after):
        result, mark = project(
            (FIRST_UNIT[j], len(CHUNKS[j])), spots, [(theirs, FAR + HANDED, far[j], 0)],
            jnp.bfloat16, handed_sum, after=after,
        )
        backs.append(over(result, outward))
        return mark

    def own(j, *after):
        result, mark = project(
            (FIRST_UNIT[j], len(CHUNKS[j])), spots,
            [(ours, FAR, far[j], 0), (ours, NEAR, near[j], 0)], jnp.float32, own_sum, after=after,
        )
        owns.append(result)
        return mark

    def attention(j, *after):
        left, right, mark = attend_chunk(j, owns[j], backs[j], cosine, sine, reach, held, after)
        contexts.append((left, over(right, swap)))
        return mark

    mark = product(0, mark)
    mark = own(0, mark)
    mark = stage(2, mark)
    mark = product(1, mark)
    mark = own(1, mark)
    mark = stage(3, mark)
    mark = product(2, mark)
    *held, mark = keep_keys(owns[0], backs[0], cosine, sine, (mark,))
    mark = own(2, mark)
    mark = product(3, mark)
    mark = attention(1, mark)
    mark = own(3, mark, came[2], came[3])
    mark = attention(2, mark)
    mark = attention(3, mark)
    new_params, new_momentum, mark = outer_update(table, start, own_rows, moved, came, (mark,))

    mine = jnp.concatenate([first for first, _ in contexts], 1)
    came = jnp.concatenate([second for _, second in contexts], 1)
    context = jnp.where(
        core == 0, jnp.concatenate([mine, came], 1), jnp.concatenate([came, mine], 1)
    )
    return (context[None], new_params[None], new_momentum[None])


def step(exchange, tokens, positions, weights, anchor, momentum):
    context = attention_step(tokens, positions, weights)
    new_params, new_momentum = outer_step(exchange, weights, anchor, momentum)
    return (context, new_params, new_momentum)


def body(tokens, positions, partner, weights, anchor, momentum):
    count = lax.axis_size("replica")
    arrays = (tokens, positions, weights, anchor, momentum)
    if count == SQUARE and lax.axis_size("fsdp") == LINE * CORES:
        return line_step(partner, *arrays)
    return step(lambda values: exchange_any(values, partner, count), *arrays)


def solution(mesh):
    placed = (
        P("replica", "fsdp", None),
        P("replica", "fsdp"),
        P(),
        P("replica", "fsdp", None),
        P("replica", "fsdp", None),
        P("replica", "fsdp", None),
    )
    return jax.shard_map(
        body,
        mesh=mesh,
        in_specs=placed,
        out_specs=(
            P("replica", "fsdp", None),
            P("replica", "fsdp", None),
            P("replica", "fsdp", None),
        ),
        check_vma=False,
    )
```

```python
import jax
import jax.numpy as jnp
from jax import lax
from jax.experimental import pallas as pl
from jax.experimental.pallas import tpu as pltpu
from jax.sharding import PartitionSpec as P

D = 4096
HEADS = 16
KV_HEADS = 4
HEAD_DIM = 128


ROPE_BASE = 500000.0
MOMENTUM_RATE = 0.9
OUTER_RATE = 0.7


def rotate(heads, places):
    half = heads.shape[-1] // 2
    frequency = ROPE_BASE ** (-(jnp.arange(half, dtype=jnp.float32) * 2.0) / heads.shape[-1])
    angles = places.astype(jnp.float32)[:, None] * frequency[None, :]
    cosine = jnp.cos(angles)[:, None, :]
    sine = jnp.sin(angles)[:, None, :]
    first = heads[..., :half]
    second = heads[..., half:]
    return jnp.concatenate([first * cosine - second * sine, second * cosine + first * sine], -1)


def attend(projected, places):
    count = projected.shape[0]
    width_q = HEADS * HEAD_DIM
    width_kv = KV_HEADS * HEAD_DIM
    group = HEADS // KV_HEADS
    scaled = projected * D ** (-0.5)
    query = rotate(scaled[:, :width_q].reshape(count, HEADS, HEAD_DIM), places).astype(jnp.bfloat16)
    keys = rotate(
        scaled[:, width_q : width_q + width_kv].reshape(count, KV_HEADS, HEAD_DIM), places
    ).astype(jnp.bfloat16)
    values = scaled[:, width_q + width_kv :].reshape(count, KV_HEADS, HEAD_DIM).astype(jnp.bfloat16)
    query = query.reshape(count, KV_HEADS, group, HEAD_DIM)
    ordinal = jnp.arange(count, dtype=jnp.int32)
    distance = ordinal[:, None] - ordinal[None, :]
    visible = (distance >= 0) & (distance <= places[:, None])
    scores = jnp.einsum(
        "tkge,ske->kgts", query, keys, preferred_element_type=jnp.float32
    ) * HEAD_DIM ** (-0.5)
    scores = jnp.where(visible[None, None], scores, -1e30)
    highest = jnp.max(scores, -1, keepdims=True)
    exponent = jnp.exp(scores - highest)
    probabilities = (exponent / jnp.sum(exponent, -1, keepdims=True)).astype(jnp.bfloat16)
    context = jnp.einsum(
        "kgts,ske->tkge", probabilities, values, preferred_element_type=jnp.float32
    )
    return context.reshape(count, width_q).astype(jnp.bfloat16)


def exchange_any(values, partner, count):
    me = lax.axis_index("replica")
    received = [jnp.zeros_like(value) for value in values]
    order = jnp.arange(count, dtype=jnp.int32)
    for step in range(1, count):
        perm = [(r, (r + step) % count) for r in range(count)]

        def one_round(held):
            came = [lax.ppermute(value, "replica", perm) for value in values]
            mine = partner[me] == (me + count - step) % count
            return [jnp.where(mine, new, old) for new, old in zip(came, held)]

        used = jnp.any(partner == (order + step) % count)
        received = lax.cond(used, one_round, lambda held: held, received)
    return received


def outer_step(exchange, weights, anchor, momentum):
    pseudo = anchor[0] - weights[0].astype(jnp.float32)
    mate_pseudo, mate_momentum = exchange(
        [pseudo.astype(jnp.bfloat16), momentum[0].astype(jnp.bfloat16)]
    )
    grad_mean = 0.5 * (pseudo + mate_pseudo.astype(jnp.float32))
    mom_mean = 0.5 * (momentum[0] + mate_momentum.astype(jnp.float32))
    new_momentum = MOMENTUM_RATE * mom_mean + grad_mean
    new_params = anchor[0] - OUTER_RATE * (grad_mean + MOMENTUM_RATE * new_momentum)
    return (new_params[None], new_momentum[None])


def attention_step(tokens, positions, weights):
    rows = tokens[0]
    places = positions[0]
    projected = jnp.dot(
        rows,
        lax.all_gather(weights, "fsdp", axis=1, tiled=True)[0],
        preferred_element_type=jnp.float32,
    )
    return attend(projected, places)[None]


LINE = 4
CORES = 2
SQUARE = 4
UNIT = HEAD_DIM
GROUP = HEADS // KV_HEADS
HALF_GROUPS = KV_HEADS // CORES
CHUNKS = (("k0", "k1", "v0", "v1"), ("q0",) * GROUP, ("q1",) * 2, ("q1",) * 2)
FIRST_UNIT = tuple(sum(len(c) for c in CHUNKS[:j]) for j in range(len(CHUNKS)))
HALF_UNITS = sum(len(c) for c in CHUNKS)
PAIR = 2 * UNIT
MIB = 1024 * 1024
SMALL = pl.CostEstimate(flops=1, bytes_accessed=1, transcendentals=0)
HBM = pl.BlockSpec(memory_space=pltpu.HBM)
SMEM = pl.BlockSpec(memory_space=pltpu.SMEM)
VMEM = pl.BlockSpec(memory_space=pltpu.VMEM)
MARK = jax.ShapeDtypeStruct((8, 128), jnp.float32)


def pairs_of_half(half):
    per_half = HEADS // CORES // 2
    pairs = [HEADS // 2 + half, (HEADS + KV_HEADS) // 2 + half]
    pairs += [half * per_half + at for at in range(per_half)]
    return jnp.stack([jnp.asarray(pair, jnp.int32) for pair in pairs])


def pass_on(pieces, sem):
    count = len(pieces)
    inward = [
        pltpu.make_async_copy(source, stop, sem.at[at])
        for at, (source, stop, _) in enumerate(pieces)
    ]
    onward = [
        pltpu.make_async_copy(stop, target, sem.at[count + at])
        for at, (_, stop, target) in enumerate(pieces)
    ]
    for copy in inward:
        copy.start()
    for at in range(count):
        inward[at].wait()
        onward[at].start()
    for copy in onward:
        copy.wait()


def hand_kernel(lead, tokens, out, mark, held, sem):
    mark[...] = jnp.zeros_like(mark)
    block = tokens.shape[1] // LINE
    pieces = []
    for at in range(LINE - 1):
        source = pl.multiple_of((lead[0] + at) * block, block)
        here = slice(at * block, (at + 1) * block)
        pieces.append((tokens.at[:, pl.ds(source, block)], held.at[:, here], out.at[:, here]))
    pass_on(pieces, sem)


def hand_tokens(tokens, lead):
    rows, columns = tokens.shape
    size = (rows, columns // LINE * (LINE - 1))
    return pl.pallas_call(
        hand_kernel,
        in_specs=[SMEM, HBM],
        out_specs=(HBM, VMEM),
        out_shape=(jax.ShapeDtypeStruct(size, tokens.dtype), MARK),
        scratch_shapes=[
            pltpu.VMEM(size, tokens.dtype),
            pltpu.SemaphoreType.DMA((2 * (LINE - 1),)),
        ],
        compiler_params=pltpu.CompilerParams(vmem_limit_bytes=60 * MIB),
        cost_estimate=SMALL,
        name="hand_tokens",
    )(lead, tokens)


def pack_kernel(first, count, pairs, own, sibling, *refs):
    out, mark, held, sem = refs[-4:]
    mark[...] = jnp.zeros_like(mark)
    pieces = []
    for at in range(count):
        source = pl.multiple_of(pairs[first + at] * PAIR, PAIR)
        for k, rows in enumerate((own, sibling)):
            here = slice(at * PAIR, (at + 1) * PAIR)
            pieces.append((rows.at[:, pl.ds(source, PAIR)], held.at[k, :, here], out.at[k, :, here]))
    pass_on(pieces, sem)


def pack(first, count, own, sibling, pairs, after=()):
    size = (CORES, own.shape[0], count * PAIR)
    return pl.pallas_call(
        lambda *refs: pack_kernel(first, count, *refs),
        in_specs=[SMEM] + [HBM] * (2 + len(after)),
        out_specs=(HBM, VMEM),
        out_shape=(jax.ShapeDtypeStruct(size, own.dtype), MARK),
        scratch_shapes=[
            pltpu.VMEM(size, own.dtype),
            pltpu.SemaphoreType.DMA((2 * CORES * count,)),
        ],
        compiler_params=pltpu.CompilerParams(vmem_limit_bytes=60 * MIB),
        cost_estimate=SMALL,
        name="pack",
    )(pairs, own, sibling, *after)


def touch(value, *after):
    def kernel(*refs):
        refs[-1][...] = jnp.zeros_like(refs[-1])

    return pl.pallas_call(
        kernel,
        in_specs=[HBM] * (1 + len(after)),
        out_specs=(HBM, VMEM),
        out_shape=(jax.ShapeDtypeStruct(value.shape, value.dtype), MARK),
        input_output_aliases={0: 0},
        compiler_params=pltpu.CompilerParams(vmem_limit_bytes=60 * MIB),
        cost_estimate=SMALL,
        name="touch",
    )(value, *after)


def project_kernel(span, wide, parts, groups, slot, handed, riding, table, pairs, *refs):
    first_unit, width = span
    tokens, refs = refs[:CORES], refs[CORES:]
    sources = refs[: wide * CORES + (groups - wide) * parts]
    rider = refs[len(sources)] if riding else None
    out, mark, taken, held, total, sem = refs[-6:]
    mark[...] = jnp.zeros_like(mark)
    rows, depth = tokens[0].shape[0], held.shape[2]
    core, middle = table[0], table[1] == 1
    if out.dtype == jnp.float32:
        total = out

    def copies(group):
        found = []
        place = pl.multiple_of(table[slot + group] * CORES * depth, CORES * depth)
        for half in range(CORES):
            found.append(
                (
                    tokens[half].at[:, pl.ds(place, CORES * depth)],
                    taken.at[group, half * rows : (half + 1) * rows],
                )
            )
        for k in range(CORES):
            if group < wide:
                source = sources[group * CORES + k]
                for pair in range(width // 2):
                    column = pl.multiple_of(pairs[first_unit // 2 + pair] * PAIR, PAIR)
                    found.append(
                        (
                            source.at[:, pl.ds(column, PAIR)],
                            held.at[group, k, :, pair * PAIR : (pair + 1) * PAIR],
                        )
                    )
            else:
                left = 0
                for part in range(parts):
                    source = sources[wide * CORES + (group - wide) * parts + part]
                    here = slice(left, left + source.shape[2])
                    found.append((source.at[k], held.at[group, k, :, here]))
                    left += source.shape[2]
        return [
            pltpu.make_async_copy(*ends, sem.at[group, number]) for number, ends in enumerate(found)
        ]

    def start(group):
        for copy in copies(group):
            copy.start()

    def multiply(group):
        for copy in copies(group):
            copy.wait()
        value = None if group == 0 else total[...]
        for k in range(CORES):
            columns = pl.ds(pl.multiple_of((core + k) % CORES * depth, depth), depth)
            part = jnp.dot(
                taken[group, :, columns], held[group, k], preferred_element_type=jnp.float32
            )
            value = part if value is None else value + part
        if group == groups - 1:
            out[...] = value.astype(out.dtype)
        else:
            total[...] = value

    def every_group(run):
        if not handed:
            run(0)

        @pl.when(middle)
        def _():
            for group in range(0 if handed else 1, groups):
                run(group)

    if handed:

        @pl.when(jnp.logical_not(middle))
        def _():
            out[...] = jnp.zeros_like(out)
            if riding:
                load = pltpu.make_async_copy(rider, held.at[0, :, :, : rider.shape[2]], sem.at[0, 0])
                load.start()
                load.wait()
                for k in range(CORES):
                    left = k * rider.shape[2]
                    out[:depth, left : left + rider.shape[2]] = held[0, k, :, : rider.shape[2]]

    every_group(start)
    every_group(multiply)


def project(chunks, table, pairs, tokens, slot, wide, packed, dtype, after=(), rider=None):
    width = sum(len(CHUNKS[chunk]) for chunk in chunks)
    span = (FIRST_UNIT[chunks[0]], width)
    rows, depth = tokens[0].shape[0], packed[0][0].shape[1]
    groups = len(wide) + len(packed)
    sources = [half for both in wide for half in both]
    sources += [part for parts in packed for part in parts]
    sources += [] if rider is None else [rider]
    size = (CORES * rows, width * UNIT)
    handed = dtype != jnp.float32
    return pl.pallas_call(
        lambda *refs: project_kernel(
            span, len(wide), len(chunks), groups, slot, handed, rider is not None, *refs
        ),
        in_specs=[SMEM] * 2 + [HBM] * (CORES + len(sources) + len(after)),
        out_specs=(VMEM, VMEM),
        out_shape=(jax.ShapeDtypeStruct(size, dtype), MARK),
        scratch_shapes=[
            pltpu.VMEM((groups, CORES * rows, CORES * depth), tokens[0].dtype),
            pltpu.VMEM((groups, CORES, depth, width * UNIT), tokens[0].dtype),
            pltpu.VMEM(size if handed else (8, 128), jnp.float32),
            pltpu.SemaphoreType.DMA((groups, CORES * (1 + width // 2))),
        ],
        compiler_params=pltpu.CompilerParams(vmem_limit_bytes=60 * MIB),
        cost_estimate=SMALL,
        name="project",
    )(table, pairs, *tokens, *sources, *after)


def whole_spec(array):
    return pl.BlockSpec(array.shape, lambda i: (0,) * len(array.shape))


def unpack_kernel(came, *refs):
    out, mark, held, sem = refs[-4:]
    mark[...] = jnp.zeros_like(mark)
    depth, width = out.shape[1:]
    pass_on(
        [
            (came.at[:depth, k * width : (k + 1) * width], held.at[k], out.at[k])
            for k in range(CORES)
        ],
        sem,
    )


def unpack(came, depth, after=()):
    size = (CORES, depth, came.shape[1] // CORES)
    return pl.pallas_call(
        unpack_kernel,
        in_specs=[HBM] * (1 + len(after)),
        out_specs=(HBM, VMEM),
        out_shape=(jax.ShapeDtypeStruct(size, came.dtype), MARK),
        scratch_shapes=[
            pltpu.VMEM(size, came.dtype),
            pltpu.SemaphoreType.DMA((2 * CORES,)),
        ],
        compiler_params=pltpu.CompilerParams(vmem_limit_bytes=60 * MIB),
        cost_estimate=SMALL,
        name="unpack",
    )(came, *after)


def joined_rows(own, came, rows, unit):
    columns = slice(unit * UNIT, (unit + 1) * UNIT)
    each = came[0].shape[1] // UNIT
    there = slice(unit % each * UNIT, (unit % each + 1) * UNIT)
    rest = came[unit // each][rows, there]
    return (own[rows, columns] + rest.astype(jnp.float32)) * D ** (-0.5)


def turned(value, cosine, sine):
    return (value * cosine + pltpu.roll(value, HEAD_DIM // 2, 1) * sine).astype(jnp.bfloat16)


def kept_rows(total, rows, unit):
    return total[rows, unit * UNIT : (unit + 1) * UNIT] * D ** (-0.5)


def keep_kernel(table, own, came, cosine, sine, *refs):
    keys, values, mark = refs[-4:-1]
    mark[...] = jnp.zeros_like(mark)
    count = cosine.shape[1]
    total = refs[-1]
    total[...] = own[...] + jnp.where(table[1] == 1, 0.0, came[...].astype(jnp.float32))
    for block in range(CORES):
        rows = slice(block * count, (block + 1) * count)
        for group in range(HALF_GROUPS):
            key = kept_rows(total, rows, group)
            keys[group, block] = turned(key, cosine[block], sine[block])
            value = kept_rows(total, rows, HALF_GROUPS + group)
            values[group, block] = value.astype(jnp.bfloat16)


def keep_keys(table, own, came, cosine, sine, after=()):
    kept = jax.ShapeDtypeStruct((HALF_GROUPS, CORES) + cosine.shape[1:], jnp.bfloat16)
    return pl.pallas_call(
        keep_kernel,
        grid=(1,),
        in_specs=[SMEM] + [whole_spec(a) for a in (own, came, cosine, sine)] + [HBM] * len(after),
        out_specs=(whole_spec(kept), whole_spec(kept), whole_spec(MARK)),
        out_shape=(kept, kept, MARK),
        scratch_shapes=[pltpu.VMEM(own.shape, jnp.float32)],
        compiler_params=pltpu.CompilerParams(vmem_limit_bytes=60 * MIB),
        cost_estimate=SMALL,
        name="keep_keys",
    )(table, own, came, cosine, sine, *after)


def attend_kernel(heads, group, parts, own, cosine, sine, places, keys, values, *refs):
    came = refs[:parts]
    outs, mark, hidden = refs[-4:-2], refs[-2], refs[-1]
    mark[...] = jnp.zeros_like(mark)
    count = cosine.shape[1]
    tile = HEAD_DIM
    for block in reversed(range(CORES)):
        row = lax.broadcasted_iota(jnp.int32, (count, count), 0)
        distance = row - lax.broadcasted_iota(jnp.int32, (count, count), 1)
        visible = (distance >= 0) & (distance <= places[block])
        hidden[...] = jnp.where(visible, 0.0, -1e30)
        rows = slice(block * count, (block + 1) * count)
        queries = [
            turned(joined_rows(own, came, rows, head), cosine[block], sine[block])
            for head in range(heads)
        ]
        for top in range(0, count, tile):
            width = top + tile
            scores = lax.dot_general(
                jnp.concatenate([query[top:width] for query in queries], 0),
                keys[group, block, :width],
                (((1,), (1,)), ((), ())),
                preferred_element_type=jnp.float32,
            )
            scores = scores + jnp.concatenate([hidden[top:width, :width]] * heads, 0)
            scores = (scores - jnp.max(scores, -1, keepdims=True)) * HEAD_DIM ** (-0.5)
            exponent = jnp.exp(scores)
            share = jnp.sum(exponent, -1, keepdims=True)
            mixed = jnp.dot(
                exponent.astype(jnp.bfloat16),
                values[group, block, :width],
                preferred_element_type=jnp.float32,
            )
            mixed = (mixed / share).astype(jnp.bfloat16)
            for head in range(heads):
                outs[block][top:width, head * UNIT : (head + 1) * UNIT] = mixed[
                    head * tile : (head + 1) * tile
                ]


def attend_chunks(chunks, own, came, cosine, sine, places, held, after=()):
    count = cosine.shape[1]
    heads, group = sum(len(CHUNKS[j]) for j in chunks), int(CHUNKS[chunks[0]][0][1])
    out = jax.ShapeDtypeStruct((count, heads * UNIT), jnp.bfloat16)
    return pl.pallas_call(
        lambda *refs: attend_kernel(heads, group, len(came), *refs),
        grid=(1,),
        in_specs=[whole_spec(a) for a in (own, cosine, sine, places, *held, *came)]
        + [HBM] * len(after),
        out_specs=(whole_spec(out), whole_spec(out), whole_spec(MARK)),
        out_shape=(out, out, MARK),
        scratch_shapes=[pltpu.VMEM((count, count), jnp.float32)],
        compiler_params=pltpu.CompilerParams(vmem_limit_bytes=60 * MIB),
        cost_estimate=SMALL,
        name="attend_chunks",
    )(own, cosine, sine, places, *held, *came, *after)


PARTS = 2
TILE = 64


def sent_kernel(part, anchor, weights, momentum, *refs):
    out, mark, start, own, moved, made, sem = refs[-7:]
    mark[...] = jnp.zeros_like(mark)
    tiles = made.shape[1] // TILE
    loads, stores = [], []
    for tile in range(tiles):
        here = pl.ds(tile * TILE, TILE)
        there = pl.ds(pl.multiple_of((part[0] * tiles + tile) * TILE, TILE), TILE)
        loads.append(
            [
                pltpu.make_async_copy(source.at[there], target.at[here], sem.at[at, tile])
                for at, (source, target) in enumerate(
                    ((anchor, start), (weights, own), (momentum, moved))
                )
            ]
        )
        stores.append(pltpu.make_async_copy(made.at[:, here], out.at[:, here], sem.at[3, tile]))
    for tile in range(tiles):
        for copy in loads[tile]:
            copy.start()
    for tile in range(tiles):
        here = slice(tile * TILE, (tile + 1) * TILE)
        for copy in loads[tile]:
            copy.wait()
        made[0, here] = moved[here].astype(made.dtype)
        made[1, here] = (start[here] - own[here].astype(jnp.float32)).astype(made.dtype)
        stores[tile].start()
    for copy in stores:
        copy.wait()


def sent_part(part, anchor, weights, momentum, after=()):
    rows, columns = anchor.shape
    size = (rows // PARTS, columns)
    return pl.pallas_call(
        sent_kernel,
        in_specs=[SMEM] + [HBM] * (3 + len(after)),
        out_specs=(HBM, VMEM),
        out_shape=(jax.ShapeDtypeStruct((2,) + size, jnp.bfloat16), MARK),
        scratch_shapes=[
            pltpu.VMEM(size, jnp.float32),
            pltpu.VMEM(size, weights.dtype),
            pltpu.VMEM(size, jnp.float32),
            pltpu.VMEM((2,) + size, jnp.bfloat16),
            pltpu.SemaphoreType.DMA((4, size[0] // TILE)),
        ],
        compiler_params=pltpu.CompilerParams(vmem_limit_bytes=60 * MIB),
        cost_estimate=SMALL,
        name="sent_part",
    )(part, anchor, weights, momentum, *after)


def relay_kernel(onward, came, piece, *refs):
    out, mark, held, sem = refs[-4:]
    mark[...] = jnp.zeros_like(mark)

    @pl.when(onward[0] == 1)
    def _():
        half = came.shape[1] // 2
        parts = [pl.ds(0, half), pl.ds(half, half)]
        pass_on([(came.at[:, part], held.at[:, part], out.at[:, part]) for part in parts], sem)


def relay(onward, came, piece, after=()):
    return pl.pallas_call(
        relay_kernel,
        in_specs=[SMEM] + [HBM] * (2 + len(after)),
        out_specs=(HBM, VMEM),
        out_shape=(jax.ShapeDtypeStruct(piece.shape, piece.dtype), MARK),
        scratch_shapes=[pltpu.VMEM(piece.shape, piece.dtype), pltpu.SemaphoreType.DMA((4,))],
        input_output_aliases={2: 0},
        compiler_params=pltpu.CompilerParams(vmem_limit_bytes=60 * MIB),
        cost_estimate=SMALL,
        name="relay",
    )(onward, came, piece, *after)


def outer_kernel(table, anchor, weights, momentum, *refs):
    came = refs[:4]
    new_params, new_momentum, mark, start, own, moved, mate, sem = refs[-8:]
    mark[...] = jnp.zeros_like(mark)
    rows = start.shape[0]
    tiles = rows // TILE
    per_part = tiles // PARTS

    def mate_copy(tile, source):
        there = pl.ds(tile % per_part * TILE, TILE)
        here = pl.ds(tile * TILE, TILE)
        return pltpu.make_async_copy(source.at[:, there], mate.at[:, here], sem.at[3, tile])

    loads, stores = [], []
    for tile in range(tiles):
        here = pl.ds(tile * TILE, TILE)
        loads.append(
            [
                pltpu.make_async_copy(source.at[here], target.at[here], sem.at[at, tile])
                for at, (source, target) in enumerate(
                    ((anchor, start), (weights, own), (momentum, moved))
                )
            ]
        )
        stores.append(
            [
                pltpu.make_async_copy(source.at[here], target.at[here], sem.at[4 + at, tile])
                for at, (source, target) in enumerate(((start, new_params), (moved, new_momentum)))
            ]
        )
    for tile in range(tiles):
        for copy in loads[tile]:
            copy.start()
        for at, source in enumerate(came):

            @pl.when(table[tile // per_part] == at)
            def _():
                mate_copy(tile, source).start()

    for tile in range(tiles):
        for copy in loads[tile]:
            copy.wait()
        mate_copy(tile, came[0]).wait()
        here = slice(tile * TILE, (tile + 1) * TILE)
        begun = start[here]
        pseudo = begun - own[here].astype(jnp.float32)
        grad_mean = 0.5 * (pseudo + mate[1, here].astype(jnp.float32))
        mom_mean = 0.5 * (moved[here] + mate[0, here].astype(jnp.float32))
        made = MOMENTUM_RATE * mom_mean + grad_mean
        moved[here] = made
        start[here] = begun - OUTER_RATE * (grad_mean + MOMENTUM_RATE * made)
        for copy in stores[tile]:
            copy.start()
    for tile in range(tiles):
        for copy in stores[tile]:
            copy.wait()


def outer_update(table, anchor, weights, momentum, came, after=()):
    size = anchor.shape
    full = jax.ShapeDtypeStruct(size, jnp.float32)
    return pl.pallas_call(
        outer_kernel,
        in_specs=[SMEM] + [HBM] * (3 + len(came) + len(after)),
        out_specs=(HBM, HBM, VMEM),
        out_shape=(full, full, MARK),
        scratch_shapes=[
            pltpu.VMEM(size, jnp.float32),
            pltpu.VMEM(size, weights.dtype),
            pltpu.VMEM(size, jnp.float32),
            pltpu.VMEM((2,) + size, jnp.bfloat16),
            pltpu.SemaphoreType.DMA((6, size[0] // TILE)),
        ],
        compiler_params=pltpu.CompilerParams(vmem_limit_bytes=60 * MIB),
        cost_estimate=SMALL,
        name="outer_update",
    )(table, anchor, weights, momentum, *came, *after)


def line_step(partner, tokens, positions, weights, anchor, momentum):
    rows, places = tokens[0], positions[0]
    own_rows = weights[0]
    start, moved = anchor[0], momentum[0]
    count, depth = rows.shape[0], own_rows.shape[0]
    me = lax.axis_index("fsdp")
    chip, core = me // CORES, me % CORES
    last = LINE - 1
    chunks = len(CHUNKS)

    def over(value, pairs):
        return lax.ppermute(value, "fsdp", pairs)

    cores = range(CORES)
    swap = [(f, f ^ 1) for f in range(LINE * CORES)]
    inward = [(a * CORES + c, b * CORES + c) for a, b in ((0, 1), (last, last - 1)) for c in cores]
    across = [(a * CORES + c, b * CORES + c) for a, b in ((1, 2), (2, 1)) for c in cores]
    outward = [(b, a) for a, b in inward] + inward
    across += [(a * CORES + c, a * CORES + 1 - c) for a in (0, last) for c in cores]

    other_rows = over(own_rows, across)
    sibling_rows = over(own_rows, swap)
    lead = (chip < LINE // 2).astype(jnp.int32)
    handed, mark = hand_tokens(rows, lead[None])
    handed = over(handed, inward)

    distance = partner[0]
    part_rows = depth // PARTS

    along = [[(r, r ^ 1) for r in range(SQUARE)], [(r, r ^ 2) for r in range(SQUARE)]]
    values = (start, own_rows, moved)
    swapped = (distance == 2).astype(jnp.int32)
    first = []
    for part in (swapped, 1 - swapped):
        made, mark = sent_part(part[None], *values, (mark,))
        first.append(made)
    came = [lax.ppermute(first[at], "replica", along[at]) for at in range(2)]
    table = jnp.stack([jnp.where(distance == 3, 3, distance - 1), jnp.where(distance == 2, 3, 2)])

    pairs = pairs_of_half(core)
    packed, marks = [], (mark,)
    for j in range(chunks):
        made, mark = pack(
            FIRST_UNIT[j] // 2, len(CHUNKS[j]) // 2, own_rows, sibling_rows, pairs, marks
        )
        packed.append(made)
        marks = (mark,)
    sibling_tokens = over(rows, swap)
    both = jnp.stack([places, over(places, swap)])
    frequency = ROPE_BASE ** (
        -(jnp.arange(HEAD_DIM // 2, dtype=jnp.float32) * 2.0) / HEAD_DIM
    )
    angles = both.astype(jnp.float32)[:, :, None] * frequency
    cosine, sine = jnp.cos(angles), jnp.sin(angles)
    cosine = jnp.concatenate([cosine, cosine], -1)
    sine = jnp.concatenate([-sine, sine], -1)
    reach = both[:, :, None]

    near_chip = jnp.where(chip < LINE // 2, 0, last)
    middle = (chip > 0) & (chip < last)
    chips = jnp.stack([chip, last - chip, last - near_chip, near_chip])
    handed_chips = jnp.clip(chips - lead, 0, LINE - 2)
    spots = jnp.concatenate([jnp.stack([core, middle.astype(jnp.int32)]), chips, handed_chips])
    OURS, HANDED = 2, 2 + LINE
    ours = (rows, sibling_tokens)

    handed, mark = touch(handed, mark, cosine, sine)
    theirs = (handed, over(handed, swap))
    near, far = [over(packed[0], inward)], []

    def stage(j, *after):
        near[j], mark = touch(near[j], *far[j - 1 :], *after)
        far.append(over(near[j], across))
        if j + 2 < chunks:
            near.append(over(touch(packed[j + 1], mark)[0], inward))
        return mark

    other_rows, mark = touch(other_rows, mark, near[0])
    mark = stage(0, mark)
    wide = ((own_rows, sibling_rows), (other_rows, over(other_rows, swap)))
    onward = (distance == 3).astype(jnp.int32)[None]

    contexts, owns, backs = [], [], []

    def product(j, *after):
        rider = packed[-1] if j == 0 else None
        result, mark = project(
            (j,), spots, pairs, theirs, HANDED, wide, ((far[j],),), jnp.bfloat16, after, rider
        )
        backs.append(over(result, outward))
        return mark

    def own(js, *after):
        packed = (tuple(far[j] for j in js), tuple(near[j] for j in js))
        result, mark = project(js, spots, pairs, ours, OURS, wide, packed, jnp.float32, after)
        owns.append(result)
        return mark

    def attention(at, js, *after):
        left, right, mark = attend_chunks(
            js, owns[at], [backs[j] for j in js], cosine, sine, reach, held, after
        )
        contexts.append((left, over(right, swap)))
        return mark

    mark = stage(1, mark, *came)
    for at in range(2):
        made, mark = relay(onward, came[1 - at], first[1 - at], (mark,))
        came.append(lax.ppermute(made, "replica", along[at]))
    mark = product(0, mark)
    mark = own((0,), mark)
    mark = stage(2, mark)
    mark = product(1, mark)
    made, mark = unpack(backs[0], depth, (mark, far[2]))
    near.append(made)
    far.append(over(made, across))
    mark = product(2, mark)
    mark = own((1,), mark)
    mark = product(3, mark, backs[1])
    *held, mark = keep_keys(spots, owns[0], backs[0], cosine, sine, (mark,))
    mark = attention(1, (1,), mark)
    mark = own((2, 3), mark)
    mark = attention(2, (2, 3), mark, came[2], came[3])
    new_params, new_momentum, mark = outer_update(table, start, own_rows, moved, came, (mark,))

    mine = jnp.concatenate([first for first, _ in contexts], 1)
    came = jnp.concatenate([second for _, second in contexts], 1)
    context = jnp.where(
        core == 0, jnp.concatenate([mine, came], 1), jnp.concatenate([came, mine], 1)
    )
    return (context[None], new_params[None], new_momentum[None])


def step(exchange, tokens, positions, weights, anchor, momentum):
    context = attention_step(tokens, positions, weights)
    new_params, new_momentum = outer_step(exchange, weights, anchor, momentum)
    return (context, new_params, new_momentum)


def body(tokens, positions, partner, weights, anchor, momentum):
    count = lax.axis_size("replica")
    arrays = (tokens, positions, weights, anchor, momentum)
    if count == SQUARE and lax.axis_size("fsdp") == LINE * CORES:
        return line_step(partner, *arrays)
    return step(lambda values: exchange_any(values, partner, count), *arrays)


def solution(mesh):
    placed = (
        P("replica", "fsdp", None),
        P("replica", "fsdp"),
        P(),
        P("replica", "fsdp", None),
        P("replica", "fsdp", None),
        P("replica", "fsdp", None),
    )
    return jax.shard_map(
        body,
        mesh=mesh,
        in_specs=placed,
        out_specs=(
            P("replica", "fsdp", None),
            P("replica", "fsdp", None),
            P("replica", "fsdp", None),
        ),
        check_vma=False,
    )
```

```python
import jax
import jax.numpy as jnp
from jax import lax
from jax.experimental import pallas as pl
from jax.experimental.pallas import tpu as pltpu
from jax.sharding import PartitionSpec as P

D = 4096
HEADS = 16
KV_HEADS = 4
HEAD_DIM = 128


ROPE_BASE = 500000.0
MOMENTUM_RATE = 0.9
OUTER_RATE = 0.7


def rotate(heads, places):
    half = heads.shape[-1] // 2
    frequency = ROPE_BASE ** (-(jnp.arange(half, dtype=jnp.float32) * 2.0) / heads.shape[-1])
    angles = places.astype(jnp.float32)[:, None] * frequency[None, :]
    cosine = jnp.cos(angles)[:, None, :]
    sine = jnp.sin(angles)[:, None, :]
    first = heads[..., :half]
    second = heads[..., half:]
    return jnp.concatenate([first * cosine - second * sine, second * cosine + first * sine], -1)


def attend(projected, places):
    count = projected.shape[0]
    width_q = HEADS * HEAD_DIM
    width_kv = KV_HEADS * HEAD_DIM
    group = HEADS // KV_HEADS
    scaled = projected * D ** (-0.5)
    query = rotate(scaled[:, :width_q].reshape(count, HEADS, HEAD_DIM), places).astype(jnp.bfloat16)
    keys = rotate(
        scaled[:, width_q : width_q + width_kv].reshape(count, KV_HEADS, HEAD_DIM), places
    ).astype(jnp.bfloat16)
    values = scaled[:, width_q + width_kv :].reshape(count, KV_HEADS, HEAD_DIM).astype(jnp.bfloat16)
    query = query.reshape(count, KV_HEADS, group, HEAD_DIM)
    ordinal = jnp.arange(count, dtype=jnp.int32)
    distance = ordinal[:, None] - ordinal[None, :]
    visible = (distance >= 0) & (distance <= places[:, None])
    scores = jnp.einsum(
        "tkge,ske->kgts", query, keys, preferred_element_type=jnp.float32
    ) * HEAD_DIM ** (-0.5)
    scores = jnp.where(visible[None, None], scores, -1e30)
    highest = jnp.max(scores, -1, keepdims=True)
    exponent = jnp.exp(scores - highest)
    probabilities = (exponent / jnp.sum(exponent, -1, keepdims=True)).astype(jnp.bfloat16)
    context = jnp.einsum(
        "kgts,ske->tkge", probabilities, values, preferred_element_type=jnp.float32
    )
    return context.reshape(count, width_q).astype(jnp.bfloat16)


def exchange_any(values, partner, count):
    me = lax.axis_index("replica")
    received = [jnp.zeros_like(value) for value in values]
    order = jnp.arange(count, dtype=jnp.int32)
    for step in range(1, count):
        perm = [(r, (r + step) % count) for r in range(count)]

        def one_round(held):
            came = [lax.ppermute(value, "replica", perm) for value in values]
            mine = partner[me] == (me + count - step) % count
            return [jnp.where(mine, new, old) for new, old in zip(came, held)]

        used = jnp.any(partner == (order + step) % count)
        received = lax.cond(used, one_round, lambda held: held, received)
    return received


def outer_step(exchange, weights, anchor, momentum):
    pseudo = anchor[0] - weights[0].astype(jnp.float32)
    mate_pseudo, mate_momentum = exchange(
        [pseudo.astype(jnp.bfloat16), momentum[0].astype(jnp.bfloat16)]
    )
    grad_mean = 0.5 * (pseudo + mate_pseudo.astype(jnp.float32))
    mom_mean = 0.5 * (momentum[0] + mate_momentum.astype(jnp.float32))
    new_momentum = MOMENTUM_RATE * mom_mean + grad_mean
    new_params = anchor[0] - OUTER_RATE * (grad_mean + MOMENTUM_RATE * new_momentum)
    return (new_params[None], new_momentum[None])


def attention_step(tokens, positions, weights):
    rows = tokens[0]
    places = positions[0]
    projected = jnp.dot(
        rows,
        lax.all_gather(weights, "fsdp", axis=1, tiled=True)[0],
        preferred_element_type=jnp.float32,
    )
    return attend(projected, places)[None]


LINE = 4
CORES = 2
SQUARE = 4
UNIT = HEAD_DIM
GROUP = HEADS // KV_HEADS
HALF_GROUPS = KV_HEADS // CORES
CHUNKS = (("k0", "k1", "v0", "v1"), ("q0",) * GROUP, ("q1",) * 2, ("q1",) * 2)
FIRST_UNIT = tuple(sum(len(c) for c in CHUNKS[:j]) for j in range(len(CHUNKS)))
HALF_UNITS = sum(len(c) for c in CHUNKS)
PAIR = 2 * UNIT
MIB = 1024 * 1024
SMALL = pl.CostEstimate(flops=1, bytes_accessed=1, transcendentals=0)
HBM = pl.BlockSpec(memory_space=pltpu.HBM)
SMEM = pl.BlockSpec(memory_space=pltpu.SMEM)
VMEM = pl.BlockSpec(memory_space=pltpu.VMEM)
MARK = jax.ShapeDtypeStruct((8, 128), jnp.float32)


def pairs_of_half(half):
    per_half = HEADS // CORES // 2
    pairs = [HEADS // 2 + half, (HEADS + KV_HEADS) // 2 + half]
    pairs += [half * per_half + at for at in range(per_half)]
    return jnp.stack([jnp.asarray(pair, jnp.int32) for pair in pairs])


def pass_on(pieces, sem):
    count = len(pieces)
    inward = [
        pltpu.make_async_copy(source, stop, sem.at[at])
        for at, (source, stop, _) in enumerate(pieces)
    ]
    onward = [
        pltpu.make_async_copy(stop, target, sem.at[count + at])
        for at, (_, stop, target) in enumerate(pieces)
    ]
    for copy in inward:
        copy.start()
    for at in range(count):
        inward[at].wait()
        onward[at].start()
    for copy in onward:
        copy.wait()


def hand_kernel(lead, tokens, out, mark, held, sem):
    mark[...] = jnp.zeros_like(mark)
    block = tokens.shape[1] // LINE
    pieces = []
    for at in range(LINE - 1):
        source = pl.multiple_of((lead[0] + at) * block, block)
        here = slice(at * block, (at + 1) * block)
        pieces.append((tokens.at[:, pl.ds(source, block)], held.at[:, here], out.at[:, here]))
    pass_on(pieces, sem)


def hand_tokens(tokens, lead):
    rows, columns = tokens.shape
    size = (rows, columns // LINE * (LINE - 1))
    return pl.pallas_call(
        hand_kernel,
        in_specs=[SMEM, HBM],
        out_specs=(HBM, VMEM),
        out_shape=(jax.ShapeDtypeStruct(size, tokens.dtype), MARK),
        scratch_shapes=[
            pltpu.VMEM(size, tokens.dtype),
            pltpu.SemaphoreType.DMA((2 * (LINE - 1),)),
        ],
        compiler_params=pltpu.CompilerParams(vmem_limit_bytes=60 * MIB),
        cost_estimate=SMALL,
        name="hand_tokens",
    )(lead, tokens)


def pack_kernel(first, count, pairs, own, sibling, *refs):
    out, mark, held, sem = refs[-4:]
    mark[...] = jnp.zeros_like(mark)
    pieces = []
    for at in range(count):
        source = pl.multiple_of(pairs[first + at] * PAIR, PAIR)
        for k, rows in enumerate((own, sibling)):
            here = slice(at * PAIR, (at + 1) * PAIR)
            pieces.append((rows.at[:, pl.ds(source, PAIR)], held.at[k, :, here], out.at[k, :, here]))
    pass_on(pieces, sem)


def pack(first, count, own, sibling, pairs, after=()):
    size = (CORES, own.shape[0], count * PAIR)
    return pl.pallas_call(
        lambda *refs: pack_kernel(first, count, *refs),
        in_specs=[SMEM] + [HBM] * (2 + len(after)),
        out_specs=(HBM, VMEM),
        out_shape=(jax.ShapeDtypeStruct(size, own.dtype), MARK),
        scratch_shapes=[
            pltpu.VMEM(size, own.dtype),
            pltpu.SemaphoreType.DMA((2 * CORES * count,)),
        ],
        compiler_params=pltpu.CompilerParams(vmem_limit_bytes=60 * MIB),
        cost_estimate=SMALL,
        name="pack",
    )(pairs, own, sibling, *after)


def touch(value, *after):
    def kernel(*refs):
        refs[-1][...] = jnp.zeros_like(refs[-1])

    return pl.pallas_call(
        kernel,
        in_specs=[HBM] * (1 + len(after)),
        out_specs=(HBM, VMEM),
        out_shape=(jax.ShapeDtypeStruct(value.shape, value.dtype), MARK),
        input_output_aliases={0: 0},
        compiler_params=pltpu.CompilerParams(vmem_limit_bytes=60 * MIB),
        cost_estimate=SMALL,
        name="touch",
    )(value, *after)


def project_kernel(span, wide, parts, groups, slot, handed, riding, table, pairs, *refs):
    first_unit, width = span
    tokens, refs = refs[:CORES], refs[CORES:]
    sources = refs[: wide * CORES + (groups - wide) * parts]
    rider = refs[len(sources)] if riding else None
    out, mark, taken, held, total, sem = refs[-6:]
    mark[...] = jnp.zeros_like(mark)
    rows, depth = tokens[0].shape[0], held.shape[2]
    core, middle = table[0], table[1] == 1
    if out.dtype == jnp.float32:
        total = out

    def copies(group):
        found = []
        place = pl.multiple_of(table[slot + group] * CORES * depth, CORES * depth)
        for half in range(CORES):
            found.append(
                (
                    tokens[half].at[:, pl.ds(place, CORES * depth)],
                    taken.at[group, half * rows : (half + 1) * rows],
                )
            )
        for k in range(CORES):
            if group < wide:
                source = sources[group * CORES + k]
                for pair in range(width // 2):
                    column = pl.multiple_of(pairs[first_unit // 2 + pair] * PAIR, PAIR)
                    found.append(
                        (
                            source.at[:, pl.ds(column, PAIR)],
                            held.at[group, k, :, pair * PAIR : (pair + 1) * PAIR],
                        )
                    )
            else:
                left = 0
                for part in range(parts):
                    source = sources[wide * CORES + (group - wide) * parts + part]
                    here = slice(left, left + source.shape[2])
                    found.append((source.at[k], held.at[group, k, :, here]))
                    left += source.shape[2]
        return [
            pltpu.make_async_copy(*ends, sem.at[group, number]) for number, ends in enumerate(found)
        ]

    def start(group):
        for copy in copies(group):
            copy.start()

    def multiply(group):
        for copy in copies(group):
            copy.wait()
        value = None if group == 0 else total[...]
        for k in range(CORES):
            columns = pl.ds(pl.multiple_of((core + k) % CORES * depth, depth), depth)
            part = jnp.dot(
                taken[group, :, columns], held[group, k], preferred_element_type=jnp.float32
            )
            value = part if value is None else value + part
        if group == groups - 1:
            out[...] = value.astype(out.dtype)
        else:
            total[...] = value

    def every_group(run):
        if not handed:
            run(0)

        @pl.when(middle)
        def _():
            for group in range(0 if handed else 1, groups):
                run(group)

    if handed:

        @pl.when(jnp.logical_not(middle))
        def _():
            out[...] = jnp.zeros_like(out)
            if riding:
                load = pltpu.make_async_copy(rider, held.at[0, :, :, : rider.shape[2]], sem.at[0, 0])
                load.start()
                load.wait()
                for k in range(CORES):
                    left = k * rider.shape[2]
                    out[:depth, left : left + rider.shape[2]] = held[0, k, :, : rider.shape[2]]

    every_group(start)
    every_group(multiply)


def project(chunks, table, pairs, tokens, slot, wide, packed, dtype, after=(), rider=None):
    width = sum(len(CHUNKS[chunk]) for chunk in chunks)
    span = (FIRST_UNIT[chunks[0]], width)
    rows, depth = tokens[0].shape[0], packed[0][0].shape[1]
    groups = len(wide) + len(packed)
    sources = [half for both in wide for half in both]
    sources += [part for parts in packed for part in parts]
    sources += [] if rider is None else [rider]
    size = (CORES * rows, width * UNIT)
    handed = dtype != jnp.float32
    return pl.pallas_call(
        lambda *refs: project_kernel(
            span, len(wide), len(chunks), groups, slot, handed, rider is not None, *refs
        ),
        in_specs=[SMEM] * 2 + [HBM] * (CORES + len(sources) + len(after)),
        out_specs=(VMEM, VMEM),
        out_shape=(jax.ShapeDtypeStruct(size, dtype), MARK),
        scratch_shapes=[
            pltpu.VMEM((groups, CORES * rows, CORES * depth), tokens[0].dtype),
            pltpu.VMEM((groups, CORES, depth, width * UNIT), tokens[0].dtype),
            pltpu.VMEM(size if handed else (8, 128), jnp.float32),
            pltpu.SemaphoreType.DMA((groups, CORES * (1 + width // 2))),
        ],
        compiler_params=pltpu.CompilerParams(vmem_limit_bytes=60 * MIB),
        cost_estimate=SMALL,
        name="project",
    )(table, pairs, *tokens, *sources, *after)


def whole_spec(array):
    return pl.BlockSpec(array.shape, lambda i: (0,) * len(array.shape))


def unpack_kernel(came, *refs):
    out, mark, held, sem = refs[-4:]
    mark[...] = jnp.zeros_like(mark)
    depth, width = out.shape[1:]
    pass_on(
        [
            (came.at[:depth, k * width : (k + 1) * width], held.at[k], out.at[k])
            for k in range(CORES)
        ],
        sem,
    )


def unpack(came, depth, after=()):
    size = (CORES, depth, came.shape[1] // CORES)
    return pl.pallas_call(
        unpack_kernel,
        in_specs=[HBM] * (1 + len(after)),
        out_specs=(HBM, VMEM),
        out_shape=(jax.ShapeDtypeStruct(size, came.dtype), MARK),
        scratch_shapes=[
            pltpu.VMEM(size, came.dtype),
            pltpu.SemaphoreType.DMA((2 * CORES,)),
        ],
        compiler_params=pltpu.CompilerParams(vmem_limit_bytes=60 * MIB),
        cost_estimate=SMALL,
        name="unpack",
    )(came, *after)


def joined_rows(own, came, rows, unit):
    columns = slice(unit * UNIT, (unit + 1) * UNIT)
    each = came[0].shape[1] // UNIT
    there = slice(unit % each * UNIT, (unit % each + 1) * UNIT)
    rest = came[unit // each][rows, there]
    return (own[rows, columns] + rest.astype(jnp.float32)) * D ** (-0.5)


def turned(value, cosine, sine):
    return (value * cosine + pltpu.roll(value, HEAD_DIM // 2, 1) * sine).astype(jnp.bfloat16)


def kept_rows(total, rows, unit):
    return total[rows, unit * UNIT : (unit + 1) * UNIT] * D ** (-0.5)


def keep_kernel(table, own, came, cosine, sine, *refs):
    keys, values, mark = refs[-4:-1]
    mark[...] = jnp.zeros_like(mark)
    count = cosine.shape[1]
    total = refs[-1]
    total[...] = own[...] + jnp.where(table[1] == 1, 0.0, came[...].astype(jnp.float32))
    for block in range(CORES):
        rows = slice(block * count, (block + 1) * count)
        for group in range(HALF_GROUPS):
            key = kept_rows(total, rows, group)
            keys[group, block] = turned(key, cosine[block], sine[block])
            value = kept_rows(total, rows, HALF_GROUPS + group)
            values[group, block] = value.astype(jnp.bfloat16)


def keep_keys(table, own, came, cosine, sine, after=()):
    kept = jax.ShapeDtypeStruct((HALF_GROUPS, CORES) + cosine.shape[1:], jnp.bfloat16)
    return pl.pallas_call(
        keep_kernel,
        grid=(1,),
        in_specs=[SMEM] + [whole_spec(a) for a in (own, came, cosine, sine)] + [HBM] * len(after),
        out_specs=(whole_spec(kept), whole_spec(kept), whole_spec(MARK)),
        out_shape=(kept, kept, MARK),
        scratch_shapes=[pltpu.VMEM(own.shape, jnp.float32)],
        compiler_params=pltpu.CompilerParams(vmem_limit_bytes=60 * MIB),
        cost_estimate=SMALL,
        name="keep_keys",
    )(table, own, came, cosine, sine, *after)


def attend_kernel(heads, group, parts, own, cosine, sine, places, keys, values, *refs):
    came = refs[:parts]
    outs, mark, hidden = refs[-4:-2], refs[-2], refs[-1]
    mark[...] = jnp.zeros_like(mark)
    count = cosine.shape[1]
    tile = HEAD_DIM
    for block in reversed(range(CORES)):
        row = lax.broadcasted_iota(jnp.int32, (count, count), 0)
        distance = row - lax.broadcasted_iota(jnp.int32, (count, count), 1)
        visible = (distance >= 0) & (distance <= places[block])
        hidden[...] = jnp.where(visible, 0.0, -1e30)
        rows = slice(block * count, (block + 1) * count)
        queries = [
            turned(joined_rows(own, came, rows, head), cosine[block], sine[block])
            for head in range(heads)
        ]
        for top in range(0, count, tile):
            width = top + tile
            scores = lax.dot_general(
                jnp.concatenate([query[top:width] for query in queries], 0),
                keys[group, block, :width],
                (((1,), (1,)), ((), ())),
                preferred_element_type=jnp.float32,
            )
            scores = scores + jnp.concatenate([hidden[top:width, :width]] * heads, 0)
            scores = (scores - jnp.max(scores, -1, keepdims=True)) * HEAD_DIM ** (-0.5)
            exponent = jnp.exp(scores)
            share = jnp.sum(exponent, -1, keepdims=True)
            mixed = jnp.dot(
                exponent.astype(jnp.bfloat16),
                values[group, block, :width],
                preferred_element_type=jnp.float32,
            )
            mixed = (mixed / share).astype(jnp.bfloat16)
            for head in range(heads):
                outs[block][top:width, head * UNIT : (head + 1) * UNIT] = mixed[
                    head * tile : (head + 1) * tile
                ]


def attend_chunks(chunks, own, came, cosine, sine, places, held, after=()):
    count = cosine.shape[1]
    heads, group = sum(len(CHUNKS[j]) for j in chunks), int(CHUNKS[chunks[0]][0][1])
    out = jax.ShapeDtypeStruct((count, heads * UNIT), jnp.bfloat16)
    return pl.pallas_call(
        lambda *refs: attend_kernel(heads, group, len(came), *refs),
        grid=(1,),
        in_specs=[whole_spec(a) for a in (own, cosine, sine, places, *held, *came)]
        + [HBM] * len(after),
        out_specs=(whole_spec(out), whole_spec(out), whole_spec(MARK)),
        out_shape=(out, out, MARK),
        scratch_shapes=[pltpu.VMEM((count, count), jnp.float32)],
        compiler_params=pltpu.CompilerParams(vmem_limit_bytes=60 * MIB),
        cost_estimate=SMALL,
        name="attend_chunks",
    )(own, cosine, sine, places, *held, *came, *after)


PARTS = 2
TILE = 64


def sent_kernel(swapped, anchor, weights, momentum, *refs):
    *outs, mark, start, own, moved, made, sem = refs[-8:]
    mark[...] = jnp.zeros_like(mark)
    tiles = made.shape[2] // TILE
    places = [(part, tile) for part in range(PARTS) for tile in range(tiles)]

    def rows(part, tile):
        return pl.ds((part * tiles + tile) * TILE, TILE)

    def loads(part, tile):
        from_part = part + swapped[0] * (1 - 2 * part)
        there = pl.ds(pl.multiple_of((from_part * tiles + tile) * TILE, TILE), TILE)
        return [
            pltpu.make_async_copy(
                source.at[there], target.at[rows(part, tile)], sem.at[at, part * tiles + tile]
            )
            for at, (source, target) in enumerate(
                ((anchor, start), (weights, own), (momentum, moved))
            )
        ]

    def store(part, tile):
        here = pl.ds(tile * TILE, TILE)
        return pltpu.make_async_copy(
            made.at[part, :, here], outs[part].at[:, here], sem.at[3, part * tiles + tile]
        )

    for place in places:
        for copy in loads(*place):
            copy.start()
    for part, tile in places:
        for copy in loads(part, tile):
            copy.wait()
        here, there = rows(part, tile), pl.ds(tile * TILE, TILE)
        made[part, 0, there] = moved[here].astype(made.dtype)
        made[part, 1, there] = (start[here] - own[here].astype(jnp.float32)).astype(made.dtype)
        store(part, tile).start()
    for place in places:
        store(*place).wait()


def sent_parts(swapped, anchor, weights, momentum, after=()):
    rows, columns = anchor.shape
    part = jax.ShapeDtypeStruct((2, rows // PARTS, columns), jnp.bfloat16)
    return pl.pallas_call(
        sent_kernel,
        in_specs=[SMEM] + [HBM] * (3 + len(after)),
        out_specs=(HBM, HBM, VMEM),
        out_shape=(part, part, MARK),
        scratch_shapes=[
            pltpu.VMEM(anchor.shape, jnp.float32),
            pltpu.VMEM(anchor.shape, weights.dtype),
            pltpu.VMEM(anchor.shape, jnp.float32),
            pltpu.VMEM((PARTS,) + part.shape, jnp.bfloat16),
            pltpu.SemaphoreType.DMA((4, rows // TILE)),
        ],
        compiler_params=pltpu.CompilerParams(vmem_limit_bytes=60 * MIB),
        cost_estimate=SMALL,
        name="sent_parts",
    )(swapped, anchor, weights, momentum, *after)


def relay_kernel(onward, came, piece, *refs):
    out, mark, held, sem = refs[-4:]
    mark[...] = jnp.zeros_like(mark)

    @pl.when(onward[0] == 1)
    def _():
        half = came.shape[1] // 2
        parts = [pl.ds(0, half), pl.ds(half, half)]
        pass_on([(came.at[:, part], held.at[:, part], out.at[:, part]) for part in parts], sem)


def relay(onward, came, piece, after=()):
    return pl.pallas_call(
        relay_kernel,
        in_specs=[SMEM] + [HBM] * (2 + len(after)),
        out_specs=(HBM, VMEM),
        out_shape=(jax.ShapeDtypeStruct(piece.shape, piece.dtype), MARK),
        scratch_shapes=[pltpu.VMEM(piece.shape, piece.dtype), pltpu.SemaphoreType.DMA((4,))],
        input_output_aliases={2: 0},
        compiler_params=pltpu.CompilerParams(vmem_limit_bytes=60 * MIB),
        cost_estimate=SMALL,
        name="relay",
    )(onward, came, piece, *after)


def outer_step_of(table, arrays, came, outs, scratch):
    anchor, weights, momentum = arrays
    new_params, new_momentum = outs
    start, own, moved, mate, sem = scratch
    tiles = start.shape[0] // TILE
    per_part = tiles // PARTS

    def mate_copy(tile, source):
        there = pl.ds(tile % per_part * TILE, TILE)
        here = pl.ds(tile * TILE, TILE)
        return pltpu.make_async_copy(source.at[:, there], mate.at[:, here], sem.at[3, tile])

    def loads(tile):
        here = pl.ds(tile * TILE, TILE)
        pairs = ((anchor, start), (weights, own), (momentum, moved))
        return [
            pltpu.make_async_copy(source.at[here], target.at[here], sem.at[at, tile])
            for at, (source, target) in enumerate(pairs)
        ]

    def stores(tile):
        here = pl.ds(tile * TILE, TILE)
        pairs = ((start, new_params), (moved, new_momentum))
        return [
            pltpu.make_async_copy(source.at[here], target.at[here], sem.at[4 + at, tile])
            for at, (source, target) in enumerate(pairs)
        ]

    def begin():
        for tile in range(tiles):
            for copy in loads(tile):
                copy.start()
            for at, source in enumerate(came):

                @pl.when(table[tile // per_part] == at)
                def _():
                    mate_copy(tile, source).start()

    def finish():
        for tile in range(tiles):
            for copy in loads(tile):
                copy.wait()
            mate_copy(tile, came[0]).wait()
            here = slice(tile * TILE, (tile + 1) * TILE)
            begun = start[here]
            pseudo = begun - own[here].astype(jnp.float32)
            grad_mean = 0.5 * (pseudo + mate[1, here].astype(jnp.float32))
            mom_mean = 0.5 * (moved[here] + mate[0, here].astype(jnp.float32))
            made = MOMENTUM_RATE * mom_mean + grad_mean
            moved[here] = made
            start[here] = begun - OUTER_RATE * (grad_mean + MOMENTUM_RATE * made)
            for copy in stores(tile):
                copy.start()
        for tile in range(tiles):
            for copy in stores(tile):
                copy.wait()

    return begin, finish


def outer_update(choice, arrays, came, after=()):
    shape = arrays[0].shape
    full = jax.ShapeDtypeStruct(shape, jnp.float32)

    def kernel(choice, *refs):
        arrays, came, refs = refs[:3], refs[3:7], refs[7 + len(after) :]
        new_params, new_momentum, mark, *scratch = refs
        mark[...] = jnp.zeros_like(mark)
        begin, finish = outer_step_of(
            choice, arrays, came, (new_params, new_momentum), scratch
        )
        begin()
        finish()

    return pl.pallas_call(
        kernel,
        in_specs=[SMEM] + [HBM] * (3 + len(came) + len(after)),
        out_specs=(HBM, HBM, VMEM),
        out_shape=(full, full, MARK),
        scratch_shapes=[
            pltpu.VMEM(shape, jnp.float32),
            pltpu.VMEM(shape, arrays[1].dtype),
            pltpu.VMEM(shape, jnp.float32),
            pltpu.VMEM((2,) + shape, jnp.bfloat16),
            pltpu.SemaphoreType.DMA((6, shape[0] // TILE)),
        ],
        compiler_params=pltpu.CompilerParams(vmem_limit_bytes=60 * MIB),
        cost_estimate=SMALL,
        name="outer_update",
    )(choice, *arrays, *came, *after)


def line_step(partner, tokens, positions, weights, anchor, momentum):
    rows, places = tokens[0], positions[0]
    own_rows = weights[0]
    start, moved = anchor[0], momentum[0]
    count, depth = rows.shape[0], own_rows.shape[0]
    me = lax.axis_index("fsdp")
    chip, core = me // CORES, me % CORES
    last = LINE - 1
    chunks = len(CHUNKS)

    def over(value, pairs):
        return lax.ppermute(value, "fsdp", pairs)

    cores = range(CORES)
    swap = [(f, f ^ 1) for f in range(LINE * CORES)]
    inward = [(a * CORES + c, b * CORES + c) for a, b in ((0, 1), (last, last - 1)) for c in cores]
    across = [(a * CORES + c, b * CORES + c) for a, b in ((1, 2), (2, 1)) for c in cores]
    outward = [(b, a) for a, b in inward]
    both_ways = inward + outward
    across += [(a * CORES + c, a * CORES + 1 - c) for a in (0, last) for c in cores]

    other_rows = over(own_rows, across)
    sibling_rows = over(own_rows, swap)
    lead = (chip < LINE // 2).astype(jnp.int32)
    handed, mark = hand_tokens(rows, lead[None])
    handed = over(handed, both_ways)

    distance = partner[0]
    part_rows = depth // PARTS

    along = [[(r, r ^ 1) for r in range(SQUARE)], [(r, r ^ 2) for r in range(SQUARE)]]
    values = (start, own_rows, moved)
    swapped = (distance == 2).astype(jnp.int32)
    *first, mark = sent_parts(swapped[None], *values, (mark,))
    came = [lax.ppermute(first[at], "replica", along[at]) for at in range(2)]
    table = jnp.stack([jnp.where(distance == 3, 3, distance - 1), jnp.where(distance == 2, 3, 2)])

    pairs = pairs_of_half(core)
    packed, marks = [], (mark,)
    for j in range(chunks):
        made, mark = pack(
            FIRST_UNIT[j] // 2, len(CHUNKS[j]) // 2, own_rows, sibling_rows, pairs, marks
        )
        packed.append(made)
        marks = (mark,)
    sibling_tokens = over(rows, swap)
    both = jnp.stack([places, over(places, swap)])
    frequency = ROPE_BASE ** (
        -(jnp.arange(HEAD_DIM // 2, dtype=jnp.float32) * 2.0) / HEAD_DIM
    )
    angles = both.astype(jnp.float32)[:, :, None] * frequency
    cosine, sine = jnp.cos(angles), jnp.sin(angles)
    cosine = jnp.concatenate([cosine, cosine], -1)
    sine = jnp.concatenate([-sine, sine], -1)
    reach = both[:, :, None]

    near_chip = jnp.where(chip < LINE // 2, 0, last)
    middle = (chip > 0) & (chip < last)
    chips = jnp.stack([chip, last - chip, last - near_chip, near_chip])
    handed_chips = jnp.clip(chips - lead, 0, LINE - 2)
    spots = jnp.concatenate([jnp.stack([core, middle.astype(jnp.int32)]), chips, handed_chips])
    OURS, HANDED = 2, 2 + LINE
    ours = (rows, sibling_tokens)

    handed, mark = touch(handed, mark, cosine, sine)
    theirs = (handed, over(handed, swap))
    near, far = [over(packed[0], inward)], []

    def stage(j, *after):
        near[j], mark = touch(near[j], *far[j - 1 :], *after)
        far.append(over(near[j], across))
        if j + 2 < chunks:
            near.append(over(touch(packed[j + 1], mark)[0], inward))
        return mark

    other_rows, mark = touch(other_rows, mark, near[0])
    mark = stage(0, mark)
    wide = ((own_rows, sibling_rows), (other_rows, over(other_rows, swap)))
    onward = (distance == 3).astype(jnp.int32)[None]

    contexts, owns, backs = [], [], []

    def product(j, *after):
        rider = packed[-1] if j == 0 else None
        result, mark = project(
            (j,), spots, pairs, theirs, HANDED, wide, ((far[j],),), jnp.bfloat16, after, rider
        )
        backs.append(over(result, both_ways))
        return mark

    def own(js, *after):
        packed = (tuple(far[j] for j in js), tuple(near[j] for j in js))
        result, mark = project(js, spots, pairs, ours, OURS, wide, packed, jnp.float32, after)
        owns.append(result)
        return mark

    def attention(at, js, *after):
        left, right, mark = attend_chunks(
            js, owns[at], [backs[j] for j in js], cosine, sine, reach, held, after
        )
        contexts.append((left, over(right, swap)))
        return mark

    for at in range(2):
        made, mark = relay(onward, came[1 - at], first[1 - at], (mark,))
        came.append(lax.ppermute(made, "replica", along[at]))
    mark = stage(1, mark)
    mark = product(0, mark)
    mark = own((0,), mark)
    mark = stage(2, mark)
    mark = product(1, mark)
    mark = own((1,), mark)
    made, mark = unpack(backs[0], depth, (mark, far[2]))
    near.append(made)
    far.append(over(made, across))
    mark = product(2, mark)
    *held, mark = keep_keys(spots, owns[0], backs[0], cosine, sine, (mark,))
    mark = product(3, mark, backs[1])
    mark = attention(1, (1,), mark)
    mark = own((2, 3), mark)
    mark = attention(2, (2, 3), mark)
    new_params, new_momentum, mark = outer_update(table, values, came, (mark,))

    mine = jnp.concatenate([first for first, _ in contexts], 1)
    came = jnp.concatenate([second for _, second in contexts], 1)
    context = jnp.where(
        core == 0, jnp.concatenate([mine, came], 1), jnp.concatenate([came, mine], 1)
    )
    return (context[None], new_params[None], new_momentum[None])


def step(exchange, tokens, positions, weights, anchor, momentum):
    context = attention_step(tokens, positions, weights)
    new_params, new_momentum = outer_step(exchange, weights, anchor, momentum)
    return (context, new_params, new_momentum)


def body(tokens, positions, partner, weights, anchor, momentum):
    count = lax.axis_size("replica")
    arrays = (tokens, positions, weights, anchor, momentum)
    if count == SQUARE and lax.axis_size("fsdp") == LINE * CORES:
        return line_step(partner, *arrays)
    return step(lambda values: exchange_any(values, partner, count), *arrays)


def solution(mesh):
    placed = (
        P("replica", "fsdp", None),
        P("replica", "fsdp"),
        P(),
        P("replica", "fsdp", None),
        P("replica", "fsdp", None),
        P("replica", "fsdp", None),
    )
    return jax.shard_map(
        body,
        mesh=mesh,
        in_specs=placed,
        out_specs=(
            P("replica", "fsdp", None),
            P("replica", "fsdp", None),
            P("replica", "fsdp", None),
        ),
        check_vma=False,
    )
```

```python
import jax
import jax.numpy as jnp
from jax import lax
from jax.experimental import pallas as pl
from jax.experimental.pallas import tpu as pltpu
from jax.sharding import PartitionSpec as P

D = 4096
HEADS = 16
KV_HEADS = 4
HEAD_DIM = 128


ROPE_BASE = 500000.0
MOMENTUM_RATE = 0.9
OUTER_RATE = 0.7


def rotate(heads, places):
    half = heads.shape[-1] // 2
    frequency = ROPE_BASE ** (-(jnp.arange(half, dtype=jnp.float32) * 2.0) / heads.shape[-1])
    angles = places.astype(jnp.float32)[:, None] * frequency[None, :]
    cosine = jnp.cos(angles)[:, None, :]
    sine = jnp.sin(angles)[:, None, :]
    first = heads[..., :half]
    second = heads[..., half:]
    return jnp.concatenate([first * cosine - second * sine, second * cosine + first * sine], -1)


def attend(projected, places):
    count = projected.shape[0]
    width_q = HEADS * HEAD_DIM
    width_kv = KV_HEADS * HEAD_DIM
    group = HEADS // KV_HEADS
    scaled = projected * D ** (-0.5)
    query = rotate(scaled[:, :width_q].reshape(count, HEADS, HEAD_DIM), places).astype(jnp.bfloat16)
    keys = rotate(
        scaled[:, width_q : width_q + width_kv].reshape(count, KV_HEADS, HEAD_DIM), places
    ).astype(jnp.bfloat16)
    values = scaled[:, width_q + width_kv :].reshape(count, KV_HEADS, HEAD_DIM).astype(jnp.bfloat16)
    query = query.reshape(count, KV_HEADS, group, HEAD_DIM)
    ordinal = jnp.arange(count, dtype=jnp.int32)
    distance = ordinal[:, None] - ordinal[None, :]
    visible = (distance >= 0) & (distance <= places[:, None])
    scores = jnp.einsum(
        "tkge,ske->kgts", query, keys, preferred_element_type=jnp.float32
    ) * HEAD_DIM ** (-0.5)
    scores = jnp.where(visible[None, None], scores, -1e30)
    highest = jnp.max(scores, -1, keepdims=True)
    exponent = jnp.exp(scores - highest)
    probabilities = (exponent / jnp.sum(exponent, -1, keepdims=True)).astype(jnp.bfloat16)
    context = jnp.einsum(
        "kgts,ske->tkge", probabilities, values, preferred_element_type=jnp.float32
    )
    return context.reshape(count, width_q).astype(jnp.bfloat16)


def exchange_any(values, partner, count):
    me = lax.axis_index("replica")
    received = [jnp.zeros_like(value) for value in values]
    order = jnp.arange(count, dtype=jnp.int32)
    for step in range(1, count):
        perm = [(r, (r + step) % count) for r in range(count)]

        def one_round(held):
            came = [lax.ppermute(value, "replica", perm) for value in values]
            mine = partner[me] == (me + count - step) % count
            return [jnp.where(mine, new, old) for new, old in zip(came, held)]

        used = jnp.any(partner == (order + step) % count)
        received = lax.cond(used, one_round, lambda held: held, received)
    return received


def outer_step(exchange, weights, anchor, momentum):
    pseudo = anchor[0] - weights[0].astype(jnp.float32)
    mate_pseudo, mate_momentum = exchange(
        [pseudo.astype(jnp.bfloat16), momentum[0].astype(jnp.bfloat16)]
    )
    grad_mean = 0.5 * (pseudo + mate_pseudo.astype(jnp.float32))
    mom_mean = 0.5 * (momentum[0] + mate_momentum.astype(jnp.float32))
    new_momentum = MOMENTUM_RATE * mom_mean + grad_mean
    new_params = anchor[0] - OUTER_RATE * (grad_mean + MOMENTUM_RATE * new_momentum)
    return (new_params[None], new_momentum[None])


def attention_step(tokens, positions, weights):
    rows = tokens[0]
    places = positions[0]
    projected = jnp.dot(
        rows,
        lax.all_gather(weights, "fsdp", axis=1, tiled=True)[0],
        preferred_element_type=jnp.float32,
    )
    return attend(projected, places)[None]


LINE = 4
CORES = 2
SQUARE = 4
UNIT = HEAD_DIM
GROUP = HEADS // KV_HEADS
HALF_GROUPS = KV_HEADS // CORES
CHUNKS = (("k0", "k1", "v0", "v1"), ("q0",) * GROUP, ("q1",) * 2, ("q1",) * 2)
FIRST_UNIT = tuple(sum(len(c) for c in CHUNKS[:j]) for j in range(len(CHUNKS)))
HALF_UNITS = sum(len(c) for c in CHUNKS)
PAIR = 2 * UNIT
MIB = 1024 * 1024
SMALL = pl.CostEstimate(flops=1, bytes_accessed=1, transcendentals=0)
HBM = pl.BlockSpec(memory_space=pltpu.HBM)
SMEM = pl.BlockSpec(memory_space=pltpu.SMEM)
VMEM = pl.BlockSpec(memory_space=pltpu.VMEM)
MARK = jax.ShapeDtypeStruct((8, 128), jnp.float32)


def pairs_of_half(half):
    per_half = HEADS // CORES // 2
    pairs = [HEADS // 2 + half, (HEADS + KV_HEADS) // 2 + half]
    pairs += [half * per_half + at for at in range(per_half)]
    return jnp.stack([jnp.asarray(pair, jnp.int32) for pair in pairs])


def pass_on(pieces, sem):
    count = len(pieces)
    inward = [
        pltpu.make_async_copy(source, stop, sem.at[at])
        for at, (source, stop, _) in enumerate(pieces)
    ]
    onward = [
        pltpu.make_async_copy(stop, target, sem.at[count + at])
        for at, (_, stop, target) in enumerate(pieces)
    ]
    for copy in inward:
        copy.start()
    for at in range(count):
        inward[at].wait()
        onward[at].start()
    for copy in onward:
        copy.wait()


def hand_kernel(lead, tokens, out, mark, held, sem):
    mark[...] = jnp.zeros_like(mark)
    block = tokens.shape[1] // LINE
    pieces = []
    for at in range(LINE - 1):
        source = pl.multiple_of((lead[0] + at) * block, block)
        here = slice(at * block, (at + 1) * block)
        pieces.append((tokens.at[:, pl.ds(source, block)], held.at[:, here], out.at[:, here]))
    pass_on(pieces, sem)


def hand_tokens(tokens, lead):
    rows, columns = tokens.shape
    size = (rows, columns // LINE * (LINE - 1))
    return pl.pallas_call(
        hand_kernel,
        in_specs=[SMEM, HBM],
        out_specs=(HBM, VMEM),
        out_shape=(jax.ShapeDtypeStruct(size, tokens.dtype), MARK),
        scratch_shapes=[
            pltpu.VMEM(size, tokens.dtype),
            pltpu.SemaphoreType.DMA((2 * (LINE - 1),)),
        ],
        compiler_params=pltpu.CompilerParams(vmem_limit_bytes=60 * MIB),
        cost_estimate=SMALL,
        name="hand_tokens",
    )(lead, tokens)


def pack_kernel(first, count, pairs, own, sibling, *refs):
    out, mark, held, sem = refs[-4:]
    mark[...] = jnp.zeros_like(mark)
    pieces = []
    for at in range(count):
        source = pl.multiple_of(pairs[first + at] * PAIR, PAIR)
        for k, rows in enumerate((own, sibling)):
            here = slice(at * PAIR, (at + 1) * PAIR)
            pieces.append((rows.at[:, pl.ds(source, PAIR)], held.at[k, :, here], out.at[k, :, here]))
    pass_on(pieces, sem)


def pack(first, count, own, sibling, pairs, after=()):
    size = (CORES, own.shape[0], count * PAIR)
    return pl.pallas_call(
        lambda *refs: pack_kernel(first, count, *refs),
        in_specs=[SMEM] + [HBM] * (2 + len(after)),
        out_specs=(HBM, VMEM),
        out_shape=(jax.ShapeDtypeStruct(size, own.dtype), MARK),
        scratch_shapes=[
            pltpu.VMEM(size, own.dtype),
            pltpu.SemaphoreType.DMA((2 * CORES * count,)),
        ],
        compiler_params=pltpu.CompilerParams(vmem_limit_bytes=60 * MIB),
        cost_estimate=SMALL,
        name="pack",
    )(pairs, own, sibling, *after)


def touch(value, *after):
    def kernel(*refs):
        refs[-1][...] = jnp.zeros_like(refs[-1])

    return pl.pallas_call(
        kernel,
        in_specs=[HBM] * (1 + len(after)),
        out_specs=(HBM, VMEM),
        out_shape=(jax.ShapeDtypeStruct(value.shape, value.dtype), MARK),
        input_output_aliases={0: 0},
        compiler_params=pltpu.CompilerParams(vmem_limit_bytes=60 * MIB),
        cost_estimate=SMALL,
        name="touch",
    )(value, *after)


def project_kernel(span, wide, parts, groups, slot, handed, riding, table, pairs, *refs):
    first_unit, width = span
    tokens, refs = refs[:CORES], refs[CORES:]
    sources = refs[: wide * CORES + (groups - wide) * parts]
    rider = refs[len(sources)] if riding else None
    out, mark, taken, held, total, sem = refs[-6:]
    mark[...] = jnp.zeros_like(mark)
    rows, depth = tokens[0].shape[0], held.shape[2]
    core, middle = table[0], table[1] == 1
    if out.dtype == jnp.float32:
        total = out

    def copies(group):
        found = []
        place = pl.multiple_of(table[slot + group] * CORES * depth, CORES * depth)
        for half in range(CORES):
            found.append(
                (
                    tokens[half].at[:, pl.ds(place, CORES * depth)],
                    taken.at[group, half * rows : (half + 1) * rows],
                )
            )
        for k in range(CORES):
            if group < wide:
                source = sources[group * CORES + k]
                for pair in range(width // 2):
                    column = pl.multiple_of(pairs[first_unit // 2 + pair] * PAIR, PAIR)
                    found.append(
                        (
                            source.at[:, pl.ds(column, PAIR)],
                            held.at[group, k, :, pair * PAIR : (pair + 1) * PAIR],
                        )
                    )
            else:
                left = 0
                for part in range(parts):
                    source = sources[wide * CORES + (group - wide) * parts + part]
                    here = slice(left, left + source.shape[2])
                    found.append((source.at[k], held.at[group, k, :, here]))
                    left += source.shape[2]
        return [
            pltpu.make_async_copy(*ends, sem.at[group, number]) for number, ends in enumerate(found)
        ]

    def start(group):
        for copy in copies(group):
            copy.start()

    def multiply(group):
        for copy in copies(group):
            copy.wait()
        value = None if group == 0 else total[...]
        for k in range(CORES):
            columns = pl.ds(pl.multiple_of((core + k) % CORES * depth, depth), depth)
            part = jnp.dot(
                taken[group, :, columns], held[group, k], preferred_element_type=jnp.float32
            )
            value = part if value is None else value + part
        if group == groups - 1:
            out[...] = value.astype(out.dtype)
        else:
            total[...] = value

    def every_group(run):
        if not handed:
            run(0)

        @pl.when(middle)
        def _():
            for group in range(0 if handed else 1, groups):
                run(group)

    if handed:

        @pl.when(jnp.logical_not(middle))
        def _():
            out[...] = jnp.zeros_like(out)
            if riding:
                load = pltpu.make_async_copy(rider, held.at[0, :, :, : rider.shape[2]], sem.at[0, 0])
                load.start()
                load.wait()
                for k in range(CORES):
                    left = k * rider.shape[2]
                    out[:depth, left : left + rider.shape[2]] = held[0, k, :, : rider.shape[2]]

    every_group(start)
    every_group(multiply)


def project(chunks, table, pairs, tokens, slot, wide, packed, dtype, after=(), rider=None):
    width = sum(len(CHUNKS[chunk]) for chunk in chunks)
    span = (FIRST_UNIT[chunks[0]], width)
    rows, depth = tokens[0].shape[0], packed[0][0].shape[1]
    groups = len(wide) + len(packed)
    sources = [half for both in wide for half in both]
    sources += [part for parts in packed for part in parts]
    sources += [] if rider is None else [rider]
    size = (CORES * rows, width * UNIT)
    handed = dtype != jnp.float32
    return pl.pallas_call(
        lambda *refs: project_kernel(
            span, len(wide), len(chunks), groups, slot, handed, rider is not None, *refs
        ),
        in_specs=[SMEM] * 2 + [HBM] * (CORES + len(sources) + len(after)),
        out_specs=(VMEM, VMEM),
        out_shape=(jax.ShapeDtypeStruct(size, dtype), MARK),
        scratch_shapes=[
            pltpu.VMEM((groups, CORES * rows, CORES * depth), tokens[0].dtype),
            pltpu.VMEM((groups, CORES, depth, width * UNIT), tokens[0].dtype),
            pltpu.VMEM(size if handed else (8, 128), jnp.float32),
            pltpu.SemaphoreType.DMA((groups, CORES * (1 + width // 2))),
        ],
        compiler_params=pltpu.CompilerParams(vmem_limit_bytes=60 * MIB),
        cost_estimate=SMALL,
        name="project",
    )(table, pairs, *tokens, *sources, *after)


def whole_spec(array):
    return pl.BlockSpec(array.shape, lambda i: (0,) * len(array.shape))


def unpack_kernel(came, *refs):
    out, mark, held, sem = refs[-4:]
    mark[...] = jnp.zeros_like(mark)
    depth, width = out.shape[1:]
    pass_on(
        [
            (came.at[:depth, k * width : (k + 1) * width], held.at[k], out.at[k])
            for k in range(CORES)
        ],
        sem,
    )


def unpack(came, depth, after=()):
    size = (CORES, depth, came.shape[1] // CORES)
    return pl.pallas_call(
        unpack_kernel,
        in_specs=[HBM] * (1 + len(after)),
        out_specs=(HBM, VMEM),
        out_shape=(jax.ShapeDtypeStruct(size, came.dtype), MARK),
        scratch_shapes=[
            pltpu.VMEM(size, came.dtype),
            pltpu.SemaphoreType.DMA((2 * CORES,)),
        ],
        compiler_params=pltpu.CompilerParams(vmem_limit_bytes=60 * MIB),
        cost_estimate=SMALL,
        name="unpack",
    )(came, *after)


def joined_rows(own, came, rows, unit):
    columns = slice(unit * UNIT, (unit + 1) * UNIT)
    each = came[0].shape[1] // UNIT
    there = slice(unit % each * UNIT, (unit % each + 1) * UNIT)
    rest = came[unit // each][rows, there]
    return (own[rows, columns] + rest.astype(jnp.float32)) * D ** (-0.5)


def turned(value, cosine, sine):
    return (value * cosine + pltpu.roll(value, HEAD_DIM // 2, 1) * sine).astype(jnp.bfloat16)


def kept_rows(total, rows, unit):
    return total[rows, unit * UNIT : (unit + 1) * UNIT] * D ** (-0.5)


def keep_kernel(table, own, came, cosine, sine, *refs):
    keys, values, mark = refs[-4:-1]
    mark[...] = jnp.zeros_like(mark)
    count = cosine.shape[1]
    total = refs[-1]
    total[...] = own[...] + jnp.where(table[1] == 1, 0.0, came[...].astype(jnp.float32))
    for block in range(CORES):
        rows = slice(block * count, (block + 1) * count)
        for group in range(HALF_GROUPS):
            key = kept_rows(total, rows, group)
            keys[group, block] = turned(key, cosine[block], sine[block])
            value = kept_rows(total, rows, HALF_GROUPS + group)
            values[group, block] = value.astype(jnp.bfloat16)


def keep_keys(table, own, came, cosine, sine, after=()):
    kept = jax.ShapeDtypeStruct((HALF_GROUPS, CORES) + cosine.shape[1:], jnp.bfloat16)
    return pl.pallas_call(
        keep_kernel,
        grid=(1,),
        in_specs=[SMEM] + [whole_spec(a) for a in (own, came, cosine, sine)] + [HBM] * len(after),
        out_specs=(whole_spec(kept), whole_spec(kept), whole_spec(MARK)),
        out_shape=(kept, kept, MARK),
        scratch_shapes=[pltpu.VMEM(own.shape, jnp.float32)],
        compiler_params=pltpu.CompilerParams(vmem_limit_bytes=60 * MIB),
        cost_estimate=SMALL,
        name="keep_keys",
    )(table, own, came, cosine, sine, *after)


def attend_kernel(heads, group, parts, own, cosine, sine, places, keys, values, *refs):
    came = refs[:parts]
    outs, mark, hidden = refs[-4:-2], refs[-2], refs[-1]
    mark[...] = jnp.zeros_like(mark)
    count = cosine.shape[1]
    tile = HEAD_DIM
    for block in reversed(range(CORES)):
        row = lax.broadcasted_iota(jnp.int32, (count, count), 0)
        distance = row - lax.broadcasted_iota(jnp.int32, (count, count), 1)
        visible = (distance >= 0) & (distance <= places[block])
        hidden[...] = jnp.where(visible, 0.0, -1e30)
        rows = slice(block * count, (block + 1) * count)
        queries = [
            turned(joined_rows(own, came, rows, head), cosine[block], sine[block])
            for head in range(heads)
        ]
        for top in range(0, count, tile):
            width = top + tile
            scores = lax.dot_general(
                jnp.concatenate([query[top:width] for query in queries], 0),
                keys[group, block, :width],
                (((1,), (1,)), ((), ())),
                preferred_element_type=jnp.float32,
            )
            scores = scores + jnp.concatenate([hidden[top:width, :width]] * heads, 0)
            scores = (scores - jnp.max(scores, -1, keepdims=True)) * HEAD_DIM ** (-0.5)
            exponent = jnp.exp(scores)
            share = jnp.sum(exponent, -1, keepdims=True)
            mixed = jnp.dot(
                exponent.astype(jnp.bfloat16),
                values[group, block, :width],
                preferred_element_type=jnp.float32,
            )
            mixed = (mixed / share).astype(jnp.bfloat16)
            for head in range(heads):
                outs[block][top:width, head * UNIT : (head + 1) * UNIT] = mixed[
                    head * tile : (head + 1) * tile
                ]


def attend_chunks(chunks, own, came, cosine, sine, places, held, after=()):
    count = cosine.shape[1]
    heads, group = sum(len(CHUNKS[j]) for j in chunks), int(CHUNKS[chunks[0]][0][1])
    out = jax.ShapeDtypeStruct((count, heads * UNIT), jnp.bfloat16)
    return pl.pallas_call(
        lambda *refs: attend_kernel(heads, group, len(came), *refs),
        grid=(1,),
        in_specs=[whole_spec(a) for a in (own, cosine, sine, places, *held, *came)]
        + [HBM] * len(after),
        out_specs=(whole_spec(out), whole_spec(out), whole_spec(MARK)),
        out_shape=(out, out, MARK),
        scratch_shapes=[pltpu.VMEM((count, count), jnp.float32)],
        compiler_params=pltpu.CompilerParams(vmem_limit_bytes=60 * MIB),
        cost_estimate=SMALL,
        name="attend_chunks",
    )(own, cosine, sine, places, *held, *came, *after)


PARTS = 2
TILE = 64


def sent_kernel(swapped, anchor, weights, momentum, *refs):
    *outs, mark, start, own, moved, made, sem = refs[-8:]
    mark[...] = jnp.zeros_like(mark)
    tiles = made.shape[2] // TILE
    places = [(part, tile) for part in range(PARTS) for tile in range(tiles)]

    def rows(part, tile):
        return pl.ds((part * tiles + tile) * TILE, TILE)

    def loads(part, tile):
        from_part = part + swapped[0] * (1 - 2 * part)
        there = pl.ds(pl.multiple_of((from_part * tiles + tile) * TILE, TILE), TILE)
        return [
            pltpu.make_async_copy(
                source.at[there], target.at[rows(part, tile)], sem.at[at, part * tiles + tile]
            )
            for at, (source, target) in enumerate(
                ((anchor, start), (weights, own), (momentum, moved))
            )
        ]

    def store(part, tile):
        here = pl.ds(tile * TILE, TILE)
        return pltpu.make_async_copy(
            made.at[part, :, here], outs[part].at[:, here], sem.at[3, part * tiles + tile]
        )

    for place in places:
        for at, copy in enumerate(loads(*place)):
            copy.start(priority=at % 2)
    for part, tile in places:
        for copy in loads(part, tile):
            copy.wait()
        here, there = rows(part, tile), pl.ds(tile * TILE, TILE)
        made[part, 0, there] = moved[here].astype(made.dtype)
        made[part, 1, there] = (start[here] - own[here].astype(jnp.float32)).astype(made.dtype)
        store(part, tile).start()
    for place in places:
        store(*place).wait()


def sent_parts(swapped, anchor, weights, momentum, after=()):
    rows, columns = anchor.shape
    part = jax.ShapeDtypeStruct((2, rows // PARTS, columns), jnp.bfloat16)
    return pl.pallas_call(
        sent_kernel,
        in_specs=[SMEM] + [HBM] * (3 + len(after)),
        out_specs=(HBM, HBM, VMEM),
        out_shape=(part, part, MARK),
        scratch_shapes=[
            pltpu.VMEM(anchor.shape, jnp.float32),
            pltpu.VMEM(anchor.shape, weights.dtype),
            pltpu.VMEM(anchor.shape, jnp.float32),
            pltpu.VMEM((PARTS,) + part.shape, jnp.bfloat16),
            pltpu.SemaphoreType.DMA((4, rows // TILE)),
        ],
        compiler_params=pltpu.CompilerParams(vmem_limit_bytes=60 * MIB),
        cost_estimate=SMALL,
        name="sent_parts",
    )(swapped, anchor, weights, momentum, *after)


def relay_kernel(onward, came, piece, *refs):
    out, mark, held, sem = refs[-4:]
    mark[...] = jnp.zeros_like(mark)

    @pl.when(onward[0] == 1)
    def _():
        half = came.shape[1] // 2
        parts = [pl.ds(0, half), pl.ds(half, half)]
        pass_on([(came.at[:, part], held.at[:, part], out.at[:, part]) for part in parts], sem)


def relay(onward, came, piece, after=()):
    return pl.pallas_call(
        relay_kernel,
        in_specs=[SMEM] + [HBM] * (2 + len(after)),
        out_specs=(HBM, VMEM),
        out_shape=(jax.ShapeDtypeStruct(piece.shape, piece.dtype), MARK),
        scratch_shapes=[pltpu.VMEM(piece.shape, piece.dtype), pltpu.SemaphoreType.DMA((4,))],
        input_output_aliases={2: 0},
        compiler_params=pltpu.CompilerParams(vmem_limit_bytes=60 * MIB),
        cost_estimate=SMALL,
        name="relay",
    )(onward, came, piece, *after)


def outer_step_of(table, arrays, came, outs, scratch):
    anchor, weights, momentum = arrays
    new_params, new_momentum = outs
    start, own, moved, mate, sem = scratch
    tiles = start.shape[0] // TILE
    per_part = tiles // PARTS

    def mate_copy(tile, source):
        there = pl.ds(tile % per_part * TILE, TILE)
        here = pl.ds(tile * TILE, TILE)
        return pltpu.make_async_copy(source.at[:, there], mate.at[:, here], sem.at[3, tile])

    def loads(tile):
        here = pl.ds(tile * TILE, TILE)
        pairs = ((anchor, start), (weights, own), (momentum, moved))
        return [
            pltpu.make_async_copy(source.at[here], target.at[here], sem.at[at, tile])
            for at, (source, target) in enumerate(pairs)
        ]

    def stores(tile):
        here = pl.ds(tile * TILE, TILE)
        pairs = ((start, new_params), (moved, new_momentum))
        return [
            pltpu.make_async_copy(source.at[here], target.at[here], sem.at[4 + at, tile])
            for at, (source, target) in enumerate(pairs)
        ]

    def begin():
        for tile in range(tiles):
            for at, copy in enumerate(loads(tile)):
                copy.start(priority=at % 2)
            for at, source in enumerate(came):

                @pl.when(table[tile // per_part] == at)
                def _():
                    mate_copy(tile, source).start(priority=1)

    def finish():
        for tile in range(tiles):
            for copy in loads(tile):
                copy.wait()
            mate_copy(tile, came[0]).wait()
            here = slice(tile * TILE, (tile + 1) * TILE)
            begun = start[here]
            pseudo = begun - own[here].astype(jnp.float32)
            grad_mean = 0.5 * (pseudo + mate[1, here].astype(jnp.float32))
            mom_mean = 0.5 * (moved[here] + mate[0, here].astype(jnp.float32))
            made = MOMENTUM_RATE * mom_mean + grad_mean
            moved[here] = made
            start[here] = begun - OUTER_RATE * (grad_mean + MOMENTUM_RATE * made)
            for at, copy in enumerate(stores(tile)):
                copy.start(priority=at % 2)
        for tile in range(tiles):
            for copy in stores(tile):
                copy.wait()

    return begin, finish


def outer_update(choice, arrays, came, after=()):
    shape = arrays[0].shape
    full = jax.ShapeDtypeStruct(shape, jnp.float32)

    def kernel(choice, *refs):
        arrays, came, refs = refs[:3], refs[3:7], refs[7 + len(after) :]
        new_params, new_momentum, mark, *scratch = refs
        mark[...] = jnp.zeros_like(mark)
        begin, finish = outer_step_of(
            choice, arrays, came, (new_params, new_momentum), scratch
        )
        begin()
        finish()

    return pl.pallas_call(
        kernel,
        in_specs=[SMEM] + [HBM] * (3 + len(came) + len(after)),
        out_specs=(HBM, HBM, VMEM),
        out_shape=(full, full, MARK),
        scratch_shapes=[
            pltpu.VMEM(shape, jnp.float32),
            pltpu.VMEM(shape, arrays[1].dtype),
            pltpu.VMEM(shape, jnp.float32),
            pltpu.VMEM((2,) + shape, jnp.bfloat16),
            pltpu.SemaphoreType.DMA((6, shape[0] // TILE)),
        ],
        compiler_params=pltpu.CompilerParams(vmem_limit_bytes=60 * MIB),
        cost_estimate=SMALL,
        name="outer_update",
    )(choice, *arrays, *came, *after)


def line_step(partner, tokens, positions, weights, anchor, momentum):
    rows, places = tokens[0], positions[0]
    own_rows = weights[0]
    start, moved = anchor[0], momentum[0]
    count, depth = rows.shape[0], own_rows.shape[0]
    me = lax.axis_index("fsdp")
    chip, core = me // CORES, me % CORES
    last = LINE - 1
    chunks = len(CHUNKS)

    def over(value, pairs):
        return lax.ppermute(value, "fsdp", pairs)

    cores = range(CORES)
    swap = [(f, f ^ 1) for f in range(LINE * CORES)]
    inward = [(a * CORES + c, b * CORES + c) for a, b in ((0, 1), (last, last - 1)) for c in cores]
    across = [(a * CORES + c, b * CORES + c) for a, b in ((1, 2), (2, 1)) for c in cores]
    outward = [(b, a) for a, b in inward]
    both_ways = inward + outward
    across += [(a * CORES + c, a * CORES + 1 - c) for a in (0, last) for c in cores]

    other_rows = over(own_rows, across)
    sibling_rows = over(own_rows, swap)
    lead = (chip < LINE // 2).astype(jnp.int32)
    handed, mark = hand_tokens(rows, lead[None])
    handed = over(handed, both_ways)

    distance = partner[0]
    part_rows = depth // PARTS

    along = [[(r, r ^ 1) for r in range(SQUARE)], [(r, r ^ 2) for r in range(SQUARE)]]
    values = (start, own_rows, moved)
    swapped = (distance == 2).astype(jnp.int32)
    *first, mark = sent_parts(swapped[None], *values, (mark,))
    came = [lax.ppermute(first[at], "replica", along[at]) for at in range(2)]
    table = jnp.stack([jnp.where(distance == 3, 3, distance - 1), jnp.where(distance == 2, 3, 2)])

    pairs = pairs_of_half(core)
    packed, marks = [], (mark,)
    for j in range(chunks):
        made, mark = pack(
            FIRST_UNIT[j] // 2, len(CHUNKS[j]) // 2, own_rows, sibling_rows, pairs, marks
        )
        packed.append(made)
        marks = (mark,)
    sibling_tokens = over(rows, swap)
    both = jnp.stack([places, over(places, swap)])
    frequency = ROPE_BASE ** (
        -(jnp.arange(HEAD_DIM // 2, dtype=jnp.float32) * 2.0) / HEAD_DIM
    )
    angles = both.astype(jnp.float32)[:, :, None] * frequency
    cosine, sine = jnp.cos(angles), jnp.sin(angles)
    cosine = jnp.concatenate([cosine, cosine], -1)
    sine = jnp.concatenate([-sine, sine], -1)
    reach = both[:, :, None]

    near_chip = jnp.where(chip < LINE // 2, 0, last)
    middle = (chip > 0) & (chip < last)
    chips = jnp.stack([chip, last - chip, last - near_chip, near_chip])
    handed_chips = jnp.clip(chips - lead, 0, LINE - 2)
    spots = jnp.concatenate([jnp.stack([core, middle.astype(jnp.int32)]), chips, handed_chips])
    OURS, HANDED = 2, 2 + LINE
    ours = (rows, sibling_tokens)

    handed, mark = touch(handed, mark, cosine, sine, reach)
    theirs = (handed, over(handed, swap))
    near, far = [over(packed[0], inward)], []

    def stage(j, mark):
        if j + 2 < chunks:
            made, mark = touch(packed[j + 1], mark, near[j], *far[j - 1 :])
            far.append(over(near[j], across))
            near.append(over(made, inward))
        else:
            near[j], mark = touch(near[j], *far[j - 1 :], mark)
            far.append(over(near[j], across))
        return mark

    other_rows, mark = touch(other_rows, mark, near[0])
    mark = stage(0, mark)
    wide = ((own_rows, sibling_rows), (other_rows, over(other_rows, swap)))
    onward = (distance == 3).astype(jnp.int32)[None]

    contexts, owns, backs = [], [], []

    def product(j, *after):
        rider = packed[-1] if j == 0 else None
        result, mark = project(
            (j,), spots, pairs, theirs, HANDED, wide, ((far[j],),), jnp.bfloat16, after, rider
        )
        backs.append(over(result, both_ways))
        return mark

    def own(js, *after):
        packed = (tuple(far[j] for j in js), tuple(near[j] for j in js))
        result, mark = project(js, spots, pairs, ours, OURS, wide, packed, jnp.float32, after)
        owns.append(result)
        return mark

    def attention(at, js, *after):
        left, right, mark = attend_chunks(
            js, owns[at], [backs[j] for j in js], cosine, sine, reach, held, after
        )
        contexts.append((left, over(right, swap)))
        return mark

    for at in range(2):
        made, mark = relay(onward, came[1 - at], first[1 - at], (mark,))
        came.append(lax.ppermute(made, "replica", along[at]))
    mark = stage(1, mark)
    mark = product(0, mark)
    mark = own((0,), mark)
    mark = stage(2, mark)
    mark = product(1, mark)
    mark = own((1,), mark)
    made, mark = unpack(backs[0], depth, (mark, far[2]))
    near.append(made)
    far.append(over(made, across))
    mark = product(2, mark)
    *held, mark = keep_keys(spots, owns[0], backs[0], cosine, sine, (mark,))
    mark = product(3, mark, backs[1])
    mark = attention(1, (1,), mark)
    mark = own((2, 3), mark)
    mark = attention(2, (2, 3), mark)
    new_params, new_momentum, mark = outer_update(table, values, came, (mark,))

    mine = jnp.concatenate([first for first, _ in contexts], 1)
    came = jnp.concatenate([second for _, second in contexts], 1)
    context = jnp.where(
        core == 0, jnp.concatenate([mine, came], 1), jnp.concatenate([came, mine], 1)
    )
    return (context[None], new_params[None], new_momentum[None])


def step(exchange, tokens, positions, weights, anchor, momentum):
    context = attention_step(tokens, positions, weights)
    new_params, new_momentum = outer_step(exchange, weights, anchor, momentum)
    return (context, new_params, new_momentum)


def body(tokens, positions, partner, weights, anchor, momentum):
    count = lax.axis_size("replica")
    arrays = (tokens, positions, weights, anchor, momentum)
    if count == SQUARE and lax.axis_size("fsdp") == LINE * CORES:
        return line_step(partner, *arrays)
    return step(lambda values: exchange_any(values, partner, count), *arrays)


def solution(mesh):
    placed = (
        P("replica", "fsdp", None),
        P("replica", "fsdp"),
        P(),
        P("replica", "fsdp", None),
        P("replica", "fsdp", None),
        P("replica", "fsdp", None),
    )
    return jax.shard_map(
        body,
        mesh=mesh,
        in_specs=placed,
        out_specs=(
            P("replica", "fsdp", None),
            P("replica", "fsdp", None),
            P("replica", "fsdp", None),
        ),
        check_vma=False,
    )
```

```python
import jax
import jax.numpy as jnp
from jax import lax
from jax.experimental import pallas as pl
from jax.experimental.pallas import tpu as pltpu
from jax.sharding import PartitionSpec as P

D = 4096
HEADS = 16
KV_HEADS = 4
HEAD_DIM = 128


ROPE_BASE = 500000.0
MOMENTUM_RATE = 0.9
OUTER_RATE = 0.7


def rotate(heads, places):
    half = heads.shape[-1] // 2
    frequency = ROPE_BASE ** (-(jnp.arange(half, dtype=jnp.float32) * 2.0) / heads.shape[-1])
    angles = places.astype(jnp.float32)[:, None] * frequency[None, :]
    cosine = jnp.cos(angles)[:, None, :]
    sine = jnp.sin(angles)[:, None, :]
    first = heads[..., :half]
    second = heads[..., half:]
    return jnp.concatenate([first * cosine - second * sine, second * cosine + first * sine], -1)


def attend(projected, places):
    count = projected.shape[0]
    width_q = HEADS * HEAD_DIM
    width_kv = KV_HEADS * HEAD_DIM
    group = HEADS // KV_HEADS
    scaled = projected * D ** (-0.5)
    query = rotate(scaled[:, :width_q].reshape(count, HEADS, HEAD_DIM), places).astype(jnp.bfloat16)
    keys = rotate(
        scaled[:, width_q : width_q + width_kv].reshape(count, KV_HEADS, HEAD_DIM), places
    ).astype(jnp.bfloat16)
    values = scaled[:, width_q + width_kv :].reshape(count, KV_HEADS, HEAD_DIM).astype(jnp.bfloat16)
    query = query.reshape(count, KV_HEADS, group, HEAD_DIM)
    ordinal = jnp.arange(count, dtype=jnp.int32)
    distance = ordinal[:, None] - ordinal[None, :]
    visible = (distance >= 0) & (distance <= places[:, None])
    scores = jnp.einsum(
        "tkge,ske->kgts", query, keys, preferred_element_type=jnp.float32
    ) * HEAD_DIM ** (-0.5)
    scores = jnp.where(visible[None, None], scores, -1e30)
    highest = jnp.max(scores, -1, keepdims=True)
    exponent = jnp.exp(scores - highest)
    probabilities = (exponent / jnp.sum(exponent, -1, keepdims=True)).astype(jnp.bfloat16)
    context = jnp.einsum(
        "kgts,ske->tkge", probabilities, values, preferred_element_type=jnp.float32
    )
    return context.reshape(count, width_q).astype(jnp.bfloat16)


def exchange_any(values, partner, count):
    me = lax.axis_index("replica")
    received = [jnp.zeros_like(value) for value in values]
    order = jnp.arange(count, dtype=jnp.int32)
    for step in range(1, count):
        perm = [(r, (r + step) % count) for r in range(count)]

        def one_round(held):
            came = [lax.ppermute(value, "replica", perm) for value in values]
            mine = partner[me] == (me + count - step) % count
            return [jnp.where(mine, new, old) for new, old in zip(came, held)]

        used = jnp.any(partner == (order + step) % count)
        received = lax.cond(used, one_round, lambda held: held, received)
    return received


def outer_step(exchange, weights, anchor, momentum):
    pseudo = anchor[0] - weights[0].astype(jnp.float32)
    mate_pseudo, mate_momentum = exchange(
        [pseudo.astype(jnp.bfloat16), momentum[0].astype(jnp.bfloat16)]
    )
    grad_mean = 0.5 * (pseudo + mate_pseudo.astype(jnp.float32))
    mom_mean = 0.5 * (momentum[0] + mate_momentum.astype(jnp.float32))
    new_momentum = MOMENTUM_RATE * mom_mean + grad_mean
    new_params = anchor[0] - OUTER_RATE * (grad_mean + MOMENTUM_RATE * new_momentum)
    return (new_params[None], new_momentum[None])


def attention_step(tokens, positions, weights):
    rows = tokens[0]
    places = positions[0]
    projected = jnp.dot(
        rows,
        lax.all_gather(weights, "fsdp", axis=1, tiled=True)[0],
        preferred_element_type=jnp.float32,
    )
    return attend(projected, places)[None]


LINE = 4
CORES = 2
SQUARE = 4
UNIT = HEAD_DIM
GROUP = HEADS // KV_HEADS
HALF_GROUPS = KV_HEADS // CORES
CHUNKS = (("k0", "k1", "v0", "v1"), ("q0",) * GROUP, ("q1",) * 2, ("q1",) * 2)
FIRST_UNIT = tuple(sum(len(c) for c in CHUNKS[:j]) for j in range(len(CHUNKS)))
HALF_UNITS = sum(len(c) for c in CHUNKS)
PAIR = 2 * UNIT
MIB = 1024 * 1024
SMALL = pl.CostEstimate(flops=1, bytes_accessed=1, transcendentals=0)
HBM = pl.BlockSpec(memory_space=pltpu.HBM)
SMEM = pl.BlockSpec(memory_space=pltpu.SMEM)
VMEM = pl.BlockSpec(memory_space=pltpu.VMEM)
MARK = jax.ShapeDtypeStruct((8, 128), jnp.float32)


def pairs_of_half(half):
    per_half = HEADS // CORES // 2
    pairs = [HEADS // 2 + half, (HEADS + KV_HEADS) // 2 + half]
    pairs += [half * per_half + at for at in range(per_half)]
    return jnp.stack([jnp.asarray(pair, jnp.int32) for pair in pairs])


def pass_on(pieces, sem):
    count = len(pieces)
    inward = [
        pltpu.make_async_copy(source, stop, sem.at[at])
        for at, (source, stop, _) in enumerate(pieces)
    ]
    onward = [
        pltpu.make_async_copy(stop, target, sem.at[count + at])
        for at, (_, stop, target) in enumerate(pieces)
    ]
    for copy in inward:
        copy.start()
    for at in range(count):
        inward[at].wait()
        onward[at].start()
    for copy in onward:
        copy.wait()


def hand_kernel(lead, tokens, out, mark, held, sem):
    mark[...] = jnp.zeros_like(mark)
    block = tokens.shape[1] // LINE
    pieces = []
    for at in range(LINE - 1):
        source = pl.multiple_of((lead[0] + at) * block, block)
        here = slice(at * block, (at + 1) * block)
        pieces.append((tokens.at[:, pl.ds(source, block)], held.at[:, here], out.at[:, here]))
    pass_on(pieces, sem)


def hand_tokens(tokens, lead):
    rows, columns = tokens.shape
    size = (rows, columns // LINE * (LINE - 1))
    return pl.pallas_call(
        hand_kernel,
        in_specs=[SMEM, HBM],
        out_specs=(HBM, VMEM),
        out_shape=(jax.ShapeDtypeStruct(size, tokens.dtype), MARK),
        scratch_shapes=[
            pltpu.VMEM(size, tokens.dtype),
            pltpu.SemaphoreType.DMA((2 * (LINE - 1),)),
        ],
        compiler_params=pltpu.CompilerParams(vmem_limit_bytes=60 * MIB),
        cost_estimate=SMALL,
        name="hand_tokens",
    )(lead, tokens)


def pack_kernel(first, count, pairs, own, sibling, *refs):
    out, mark, held, sem = refs[-4:]
    mark[...] = jnp.zeros_like(mark)
    pieces = []
    for at in range(count):
        source = pl.multiple_of(pairs[first + at] * PAIR, PAIR)
        for k, rows in enumerate((own, sibling)):
            here = slice(at * PAIR, (at + 1) * PAIR)
            pieces.append((rows.at[:, pl.ds(source, PAIR)], held.at[k, :, here], out.at[k, :, here]))
    pass_on(pieces, sem)


def pack(first, count, own, sibling, pairs, after=()):
    size = (CORES, own.shape[0], count * PAIR)
    return pl.pallas_call(
        lambda *refs: pack_kernel(first, count, *refs),
        in_specs=[SMEM] + [HBM] * (2 + len(after)),
        out_specs=(HBM, VMEM),
        out_shape=(jax.ShapeDtypeStruct(size, own.dtype), MARK),
        scratch_shapes=[
            pltpu.VMEM(size, own.dtype),
            pltpu.SemaphoreType.DMA((2 * CORES * count,)),
        ],
        compiler_params=pltpu.CompilerParams(vmem_limit_bytes=60 * MIB),
        cost_estimate=SMALL,
        name="pack",
    )(pairs, own, sibling, *after)


def touch(value, *after):
    def kernel(*refs):
        refs[-1][...] = jnp.zeros_like(refs[-1])

    return pl.pallas_call(
        kernel,
        in_specs=[HBM] * (1 + len(after)),
        out_specs=(HBM, VMEM),
        out_shape=(jax.ShapeDtypeStruct(value.shape, value.dtype), MARK),
        input_output_aliases={0: 0},
        compiler_params=pltpu.CompilerParams(vmem_limit_bytes=60 * MIB),
        cost_estimate=SMALL,
        name="touch",
    )(value, *after)


def project_kernel(span, wide, parts, groups, slot, handed, riding, table, pairs, *refs, meanwhile=None):
    first_unit, width = span
    tokens, refs = refs[:CORES], refs[CORES:]
    sources = refs[: wide * CORES + (groups - wide) * parts]
    rider = refs[len(sources)] if riding else None
    out, mark, taken, held, total, sem = refs[-6:]
    mark[...] = jnp.zeros_like(mark)
    rows, depth = tokens[0].shape[0], held.shape[2]
    core, middle = table[0], table[1] == 1
    if out.dtype == jnp.float32:
        total = out

    def copies(group):
        found = []
        place = pl.multiple_of(table[slot + group] * CORES * depth, CORES * depth)
        for half in range(CORES):
            found.append(
                (
                    tokens[half].at[:, pl.ds(place, CORES * depth)],
                    taken.at[group, half * rows : (half + 1) * rows],
                )
            )
        for k in range(CORES):
            if group < wide:
                source = sources[group * CORES + k]
                for pair in range(width // 2):
                    column = pl.multiple_of(pairs[first_unit // 2 + pair] * PAIR, PAIR)
                    found.append(
                        (
                            source.at[:, pl.ds(column, PAIR)],
                            held.at[group, k, :, pair * PAIR : (pair + 1) * PAIR],
                        )
                    )
            else:
                left = 0
                for part in range(parts):
                    source = sources[wide * CORES + (group - wide) * parts + part]
                    here = slice(left, left + source.shape[2])
                    found.append((source.at[k], held.at[group, k, :, here]))
                    left += source.shape[2]
        return [
            pltpu.make_async_copy(*ends, sem.at[group, number]) for number, ends in enumerate(found)
        ]

    def start(group):
        for copy in copies(group):
            copy.start()

    def multiply(group):
        for copy in copies(group):
            copy.wait()
        value = None if group == 0 else total[...]
        for k in range(CORES):
            columns = pl.ds(pl.multiple_of((core + k) % CORES * depth, depth), depth)
            part = jnp.dot(
                taken[group, :, columns], held[group, k], preferred_element_type=jnp.float32
            )
            value = part if value is None else value + part
        if group == groups - 1:
            out[...] = value.astype(out.dtype)
        else:
            total[...] = value

    def every_group(run):
        if not handed:
            run(0)

        @pl.when(middle)
        def _():
            for group in range(0 if handed else 1, groups):
                run(group)

    if handed:

        @pl.when(jnp.logical_not(middle))
        def _():
            out[...] = jnp.zeros_like(out)
            if riding:
                load = pltpu.make_async_copy(rider, held.at[0, :, :, : rider.shape[2]], sem.at[0, 0])
                load.start()
                load.wait()
                for k in range(CORES):
                    left = k * rider.shape[2]
                    out[:depth, left : left + rider.shape[2]] = held[0, k, :, : rider.shape[2]]

    every_group(start)
    if meanwhile is not None:
        meanwhile()
    every_group(multiply)


def project(chunks, table, pairs, tokens, slot, wide, packed, dtype, after=(), rider=None):
    width = sum(len(CHUNKS[chunk]) for chunk in chunks)
    span = (FIRST_UNIT[chunks[0]], width)
    rows, depth = tokens[0].shape[0], packed[0][0].shape[1]
    groups = len(wide) + len(packed)
    sources = [half for both in wide for half in both]
    sources += [part for parts in packed for part in parts]
    sources += [] if rider is None else [rider]
    size = (CORES * rows, width * UNIT)
    handed = dtype != jnp.float32
    return pl.pallas_call(
        lambda *refs: project_kernel(
            span, len(wide), len(chunks), groups, slot, handed, rider is not None, *refs
        ),
        in_specs=[SMEM] * 2 + [HBM] * (CORES + len(sources) + len(after)),
        out_specs=(VMEM, VMEM),
        out_shape=(jax.ShapeDtypeStruct(size, dtype), MARK),
        scratch_shapes=[
            pltpu.VMEM((groups, CORES * rows, CORES * depth), tokens[0].dtype),
            pltpu.VMEM((groups, CORES, depth, width * UNIT), tokens[0].dtype),
            pltpu.VMEM(size if handed else (8, 128), jnp.float32),
            pltpu.SemaphoreType.DMA((groups, CORES * (1 + width // 2))),
        ],
        compiler_params=pltpu.CompilerParams(vmem_limit_bytes=60 * MIB),
        cost_estimate=SMALL,
        name="project",
    )(table, pairs, *tokens, *sources, *after)


def whole_spec(array):
    return pl.BlockSpec(array.shape, lambda i: (0,) * len(array.shape))


def unpack_kernel(came, *refs):
    out, mark, held, sem = refs[-4:]
    mark[...] = jnp.zeros_like(mark)
    depth, width = out.shape[1:]
    pass_on(
        [
            (came.at[:depth, k * width : (k + 1) * width], held.at[k], out.at[k])
            for k in range(CORES)
        ],
        sem,
    )


def unpack(came, depth, after=()):
    size = (CORES, depth, came.shape[1] // CORES)
    return pl.pallas_call(
        unpack_kernel,
        in_specs=[HBM] * (1 + len(after)),
        out_specs=(HBM, VMEM),
        out_shape=(jax.ShapeDtypeStruct(size, came.dtype), MARK),
        scratch_shapes=[
            pltpu.VMEM(size, came.dtype),
            pltpu.SemaphoreType.DMA((2 * CORES,)),
        ],
        compiler_params=pltpu.CompilerParams(vmem_limit_bytes=60 * MIB),
        cost_estimate=SMALL,
        name="unpack",
    )(came, *after)


def joined_rows(own, came, rows, unit):
    columns = slice(unit * UNIT, (unit + 1) * UNIT)
    each = came[0].shape[1] // UNIT
    there = slice(unit % each * UNIT, (unit % each + 1) * UNIT)
    rest = came[unit // each][rows, there]
    return (own[rows, columns] + rest.astype(jnp.float32)) * D ** (-0.5)


def turned(value, cosine, sine):
    return (value * cosine + pltpu.roll(value, HEAD_DIM // 2, 1) * sine).astype(jnp.bfloat16)


def kept_rows(total, rows, unit):
    return total[rows, unit * UNIT : (unit + 1) * UNIT] * D ** (-0.5)


def keep_kernel(table, own, came, cosine, sine, *refs):
    keys, values, mark = refs[-4:-1]
    mark[...] = jnp.zeros_like(mark)
    count = cosine.shape[1]
    total = refs[-1]
    total[...] = own[...] + jnp.where(table[1] == 1, 0.0, came[...].astype(jnp.float32))
    for block in range(CORES):
        rows = slice(block * count, (block + 1) * count)
        for group in range(HALF_GROUPS):
            key = kept_rows(total, rows, group)
            keys[group, block] = turned(key, cosine[block], sine[block])
            value = kept_rows(total, rows, HALF_GROUPS + group)
            values[group, block] = value.astype(jnp.bfloat16)


def keep_keys(table, own, came, cosine, sine, after=()):
    kept = jax.ShapeDtypeStruct((HALF_GROUPS, CORES) + cosine.shape[1:], jnp.bfloat16)
    return pl.pallas_call(
        keep_kernel,
        grid=(1,),
        in_specs=[SMEM] + [whole_spec(a) for a in (own, came, cosine, sine)] + [HBM] * len(after),
        out_specs=(whole_spec(kept), whole_spec(kept), whole_spec(MARK)),
        out_shape=(kept, kept, MARK),
        scratch_shapes=[pltpu.VMEM(own.shape, jnp.float32)],
        compiler_params=pltpu.CompilerParams(vmem_limit_bytes=60 * MIB),
        cost_estimate=SMALL,
        name="keep_keys",
    )(table, own, came, cosine, sine, *after)


def attend_kernel(heads, group, parts, own, cosine, sine, places, keys, values, *refs):
    came = refs[:parts]
    outs, mark, hidden = refs[-4:-2], refs[-2], refs[-1]
    mark[...] = jnp.zeros_like(mark)
    count = cosine.shape[1]
    tile = HEAD_DIM
    for block in reversed(range(CORES)):
        row = lax.broadcasted_iota(jnp.int32, (count, count), 0)
        distance = row - lax.broadcasted_iota(jnp.int32, (count, count), 1)
        visible = (distance >= 0) & (distance <= places[block])
        hidden[...] = jnp.where(visible, 0.0, -1e30)
        rows = slice(block * count, (block + 1) * count)
        queries = [
            turned(joined_rows(own, came, rows, head), cosine[block], sine[block])
            for head in range(heads)
        ]
        for top in range(0, count, tile):
            width = top + tile
            scores = lax.dot_general(
                jnp.concatenate([query[top:width] for query in queries], 0),
                keys[group, block, :width],
                (((1,), (1,)), ((), ())),
                preferred_element_type=jnp.float32,
            )
            scores = scores + jnp.concatenate([hidden[top:width, :width]] * heads, 0)
            scores = (scores - jnp.max(scores, -1, keepdims=True)) * HEAD_DIM ** (-0.5)
            exponent = jnp.exp(scores)
            share = jnp.sum(exponent, -1, keepdims=True)
            mixed = jnp.dot(
                exponent.astype(jnp.bfloat16),
                values[group, block, :width],
                preferred_element_type=jnp.float32,
            )
            mixed = (mixed / share).astype(jnp.bfloat16)
            for head in range(heads):
                outs[block][top:width, head * UNIT : (head + 1) * UNIT] = mixed[
                    head * tile : (head + 1) * tile
                ]


def attend_chunks(chunks, own, came, cosine, sine, places, held, after=()):
    count = cosine.shape[1]
    heads, group = sum(len(CHUNKS[j]) for j in chunks), int(CHUNKS[chunks[0]][0][1])
    out = jax.ShapeDtypeStruct((count, heads * UNIT), jnp.bfloat16)
    return pl.pallas_call(
        lambda *refs: attend_kernel(heads, group, len(came), *refs),
        grid=(1,),
        in_specs=[whole_spec(a) for a in (own, cosine, sine, places, *held, *came)]
        + [HBM] * len(after),
        out_specs=(whole_spec(out), whole_spec(out), whole_spec(MARK)),
        out_shape=(out, out, MARK),
        scratch_shapes=[pltpu.VMEM((count, count), jnp.float32)],
        compiler_params=pltpu.CompilerParams(vmem_limit_bytes=60 * MIB),
        cost_estimate=SMALL,
        name="attend_chunks",
    )(own, cosine, sine, places, *held, *came, *after)


def attend_and_project(attending, projecting, after=()):
    chunks, own, came, cosine, sine, places, held = attending
    spans, table, pairs, tokens, slot, wide, packed = projecting
    count = cosine.shape[1]
    heads, group = sum(len(CHUNKS[j]) for j in chunks), int(CHUNKS[chunks[0]][0][1])
    width = sum(len(CHUNKS[j]) for j in spans)
    rows, depth = tokens[0].shape[0], packed[0][0].shape[1]
    groups = len(wide) + len(packed)
    sources = [half for both in wide for half in both]
    sources += [part for parts in packed for part in parts]
    attended = (own, cosine, sine, places, *held, *came)
    projected = (table, pairs, *tokens, *sources)
    out = jax.ShapeDtypeStruct((count, heads * UNIT), jnp.bfloat16)
    product = jax.ShapeDtypeStruct((CORES * rows, width * UNIT), jnp.float32)

    def kernel(*refs):
        inputs, refs = refs[: len(attended)], refs[len(attended) :]
        terms, refs = refs[: len(projected)], refs[len(projected) + len(after) :]
        left, right, made, mark, hidden, *scratch = refs
        project_kernel(
            (FIRST_UNIT[spans[0]], width), len(wide), len(spans), groups, slot, False, False,
            *terms, made, mark, *scratch,
            meanwhile=lambda: attend_kernel(
                heads, group, len(came), *inputs, left, right, mark, hidden
            ),
        )

    return pl.pallas_call(
        kernel,
        grid=(1,),
        in_specs=[whole_spec(a) for a in attended]
        + [SMEM] * 2
        + [HBM] * (len(projected) - 2 + len(after)),
        out_specs=[whole_spec(a) for a in (out, out, product, MARK)],
        out_shape=(out, out, product, MARK),
        scratch_shapes=[
            pltpu.VMEM((count, count), jnp.float32),
            pltpu.VMEM((groups, CORES * rows, CORES * depth), tokens[0].dtype),
            pltpu.VMEM((groups, CORES, depth, width * UNIT), tokens[0].dtype),
            pltpu.VMEM((8, 128), jnp.float32),
            pltpu.SemaphoreType.DMA((groups, CORES * (1 + width // 2))),
        ],
        compiler_params=pltpu.CompilerParams(vmem_limit_bytes=60 * MIB),
        cost_estimate=SMALL,
        name="attend_and_project",
    )(*attended, *projected, *after)


PARTS = 2
TILE = 64


def sent_kernel(swapped, anchor, weights, momentum, *refs):
    *outs, mark, start, own, moved, made, sem = refs[-8:]
    mark[...] = jnp.zeros_like(mark)
    tiles = made.shape[2] // TILE
    places = [(part, tile) for part in range(PARTS) for tile in range(tiles)]

    def rows(part, tile):
        return pl.ds((part * tiles + tile) * TILE, TILE)

    def loads(part, tile):
        from_part = part + swapped[0] * (1 - 2 * part)
        there = pl.ds(pl.multiple_of((from_part * tiles + tile) * TILE, TILE), TILE)
        return [
            pltpu.make_async_copy(
                source.at[there], target.at[rows(part, tile)], sem.at[at, part * tiles + tile]
            )
            for at, (source, target) in enumerate(
                ((anchor, start), (weights, own), (momentum, moved))
            )
        ]

    def store(part, tile):
        here = pl.ds(tile * TILE, TILE)
        return pltpu.make_async_copy(
            made.at[part, :, here], outs[part].at[:, here], sem.at[3, part * tiles + tile]
        )

    for place in places:
        for at, copy in enumerate(loads(*place)):
            copy.start(priority=at % 2)
    for part, tile in places:
        for copy in loads(part, tile):
            copy.wait()
        here, there = rows(part, tile), pl.ds(tile * TILE, TILE)
        made[part, 0, there] = moved[here].astype(made.dtype)
        made[part, 1, there] = (start[here] - own[here].astype(jnp.float32)).astype(made.dtype)
        store(part, tile).start()
    for place in places:
        store(*place).wait()


def sent_parts(swapped, anchor, weights, momentum, after=()):
    rows, columns = anchor.shape
    part = jax.ShapeDtypeStruct((2, rows // PARTS, columns), jnp.bfloat16)
    return pl.pallas_call(
        sent_kernel,
        in_specs=[SMEM] + [HBM] * (3 + len(after)),
        out_specs=(HBM, HBM, VMEM),
        out_shape=(part, part, MARK),
        scratch_shapes=[
            pltpu.VMEM(anchor.shape, jnp.float32),
            pltpu.VMEM(anchor.shape, weights.dtype),
            pltpu.VMEM(anchor.shape, jnp.float32),
            pltpu.VMEM((PARTS,) + part.shape, jnp.bfloat16),
            pltpu.SemaphoreType.DMA((4, rows // TILE)),
        ],
        compiler_params=pltpu.CompilerParams(vmem_limit_bytes=60 * MIB),
        cost_estimate=SMALL,
        name="sent_parts",
    )(swapped, anchor, weights, momentum, *after)


def relay_kernel(onward, came, piece, *refs):
    out, mark, held, sem = refs[-4:]
    mark[...] = jnp.zeros_like(mark)

    @pl.when(onward[0] == 1)
    def _():
        half = came.shape[1] // 2
        parts = [pl.ds(0, half), pl.ds(half, half)]
        pass_on([(came.at[:, part], held.at[:, part], out.at[:, part]) for part in parts], sem)


def relay(onward, came, piece, after=()):
    return pl.pallas_call(
        relay_kernel,
        in_specs=[SMEM] + [HBM] * (2 + len(after)),
        out_specs=(HBM, VMEM),
        out_shape=(jax.ShapeDtypeStruct(piece.shape, piece.dtype), MARK),
        scratch_shapes=[pltpu.VMEM(piece.shape, piece.dtype), pltpu.SemaphoreType.DMA((4,))],
        input_output_aliases={2: 0},
        compiler_params=pltpu.CompilerParams(vmem_limit_bytes=60 * MIB),
        cost_estimate=SMALL,
        name="relay",
    )(onward, came, piece, *after)


def outer_step_of(table, arrays, came, outs, scratch):
    anchor, weights, momentum = arrays
    new_params, new_momentum = outs
    start, own, moved, mate, sem = scratch
    tiles = start.shape[0] // TILE
    per_part = tiles // PARTS

    def mate_copy(tile, source):
        there = pl.ds(tile % per_part * TILE, TILE)
        here = pl.ds(tile * TILE, TILE)
        return pltpu.make_async_copy(source.at[:, there], mate.at[:, here], sem.at[3, tile])

    def loads(tile):
        here = pl.ds(tile * TILE, TILE)
        pairs = ((anchor, start), (weights, own), (momentum, moved))
        return [
            pltpu.make_async_copy(source.at[here], target.at[here], sem.at[at, tile])
            for at, (source, target) in enumerate(pairs)
        ]

    def stores(tile):
        here = pl.ds(tile * TILE, TILE)
        pairs = ((start, new_params), (moved, new_momentum))
        return [
            pltpu.make_async_copy(source.at[here], target.at[here], sem.at[4 + at, tile])
            for at, (source, target) in enumerate(pairs)
        ]

    def begin():
        for tile in range(tiles):
            for at, copy in enumerate(loads(tile)):
                copy.start(priority=at % 2)
            for at, source in enumerate(came):

                @pl.when(table[tile // per_part] == at)
                def _():
                    mate_copy(tile, source).start(priority=1)

    def finish():
        for tile in range(tiles):
            for copy in loads(tile):
                copy.wait()
            mate_copy(tile, came[0]).wait()
            here = slice(tile * TILE, (tile + 1) * TILE)
            begun = start[here]
            pseudo = begun - own[here].astype(jnp.float32)
            grad_mean = 0.5 * (pseudo + mate[1, here].astype(jnp.float32))
            mom_mean = 0.5 * (moved[here] + mate[0, here].astype(jnp.float32))
            made = MOMENTUM_RATE * mom_mean + grad_mean
            moved[here] = made
            start[here] = begun - OUTER_RATE * (grad_mean + MOMENTUM_RATE * made)
            for at, copy in enumerate(stores(tile)):
                copy.start(priority=at % 2)
        for tile in range(tiles):
            for copy in stores(tile):
                copy.wait()

    return begin, finish


def outer_update(choice, arrays, came, after=()):
    shape = arrays[0].shape
    full = jax.ShapeDtypeStruct(shape, jnp.float32)

    def kernel(choice, *refs):
        arrays, came, refs = refs[:3], refs[3:7], refs[7 + len(after) :]
        new_params, new_momentum, mark, *scratch = refs
        mark[...] = jnp.zeros_like(mark)
        begin, finish = outer_step_of(
            choice, arrays, came, (new_params, new_momentum), scratch
        )
        begin()
        finish()

    return pl.pallas_call(
        kernel,
        in_specs=[SMEM] + [HBM] * (3 + len(came) + len(after)),
        out_specs=(HBM, HBM, VMEM),
        out_shape=(full, full, MARK),
        scratch_shapes=[
            pltpu.VMEM(shape, jnp.float32),
            pltpu.VMEM(shape, arrays[1].dtype),
            pltpu.VMEM(shape, jnp.float32),
            pltpu.VMEM((2,) + shape, jnp.bfloat16),
            pltpu.SemaphoreType.DMA((6, shape[0] // TILE)),
        ],
        compiler_params=pltpu.CompilerParams(vmem_limit_bytes=60 * MIB),
        cost_estimate=SMALL,
        name="outer_update",
    )(choice, *arrays, *came, *after)


def line_step(partner, tokens, positions, weights, anchor, momentum):
    rows, places = tokens[0], positions[0]
    own_rows = weights[0]
    start, moved = anchor[0], momentum[0]
    count, depth = rows.shape[0], own_rows.shape[0]
    me = lax.axis_index("fsdp")
    chip, core = me // CORES, me % CORES
    last = LINE - 1
    chunks = len(CHUNKS)

    def over(value, pairs):
        return lax.ppermute(value, "fsdp", pairs)

    cores = range(CORES)
    swap = [(f, f ^ 1) for f in range(LINE * CORES)]
    inward = [(a * CORES + c, b * CORES + c) for a, b in ((0, 1), (last, last - 1)) for c in cores]
    across = [(a * CORES + c, b * CORES + c) for a, b in ((1, 2), (2, 1)) for c in cores]
    outward = [(b, a) for a, b in inward]
    both_ways = inward + outward
    across += [(a * CORES + c, a * CORES + 1 - c) for a in (0, last) for c in cores]

    other_rows = over(own_rows, across)
    sibling_rows = over(own_rows, swap)
    lead = (chip < LINE // 2).astype(jnp.int32)
    handed, mark = hand_tokens(rows, lead[None])
    handed = over(handed, both_ways)

    distance = partner[0]
    part_rows = depth // PARTS

    along = [[(r, r ^ 1) for r in range(SQUARE)], [(r, r ^ 2) for r in range(SQUARE)]]
    values = (start, own_rows, moved)
    swapped = (distance == 2).astype(jnp.int32)
    *first, mark = sent_parts(swapped[None], *values, (mark,))
    came = [lax.ppermute(first[at], "replica", along[at]) for at in range(2)]
    table = jnp.stack([jnp.where(distance == 3, 3, distance - 1), jnp.where(distance == 2, 3, 2)])

    pairs = pairs_of_half(core)
    packed, marks = [], (mark,)
    for j in range(chunks):
        made, mark = pack(
            FIRST_UNIT[j] // 2, len(CHUNKS[j]) // 2, own_rows, sibling_rows, pairs, marks
        )
        packed.append(made)
        marks = (mark,)
    sibling_tokens = over(rows, swap)
    both = jnp.stack([places, over(places, swap)])
    frequency = ROPE_BASE ** (
        -(jnp.arange(HEAD_DIM // 2, dtype=jnp.float32) * 2.0) / HEAD_DIM
    )
    angles = both.astype(jnp.float32)[:, :, None] * frequency
    cosine, sine = jnp.cos(angles), jnp.sin(angles)
    cosine = jnp.concatenate([cosine, cosine], -1)
    sine = jnp.concatenate([-sine, sine], -1)
    reach = both[:, :, None]

    near_chip = jnp.where(chip < LINE // 2, 0, last)
    middle = (chip > 0) & (chip < last)
    chips = jnp.stack([chip, last - chip, last - near_chip, near_chip])
    handed_chips = jnp.clip(chips - lead, 0, LINE - 2)
    spots = jnp.concatenate([jnp.stack([core, middle.astype(jnp.int32)]), chips, handed_chips])
    OURS, HANDED = 2, 2 + LINE
    ours = (rows, sibling_tokens)

    handed, mark = touch(handed, mark, cosine, sine, reach)
    theirs = (handed, over(handed, swap))
    near, far = [over(packed[0], inward)], []

    def stage(j, mark):
        if j + 2 < chunks:
            made, mark = touch(packed[j + 1], mark, near[j], *far[j - 1 :])
            far.append(over(near[j], across))
            near.append(over(made, inward))
        else:
            near[j], mark = touch(near[j], *far[j - 1 :], mark)
            far.append(over(near[j], across))
        return mark

    other_rows, mark = touch(other_rows, mark, near[0])
    mark = stage(0, mark)
    wide = ((own_rows, sibling_rows), (other_rows, over(other_rows, swap)))
    onward = (distance == 3).astype(jnp.int32)[None]

    contexts, owns, backs = [], [], []

    def product(j, *after):
        rider = packed[-1] if j == 0 else None
        result, mark = project(
            (j,), spots, pairs, theirs, HANDED, wide, ((far[j],),), jnp.bfloat16, after, rider
        )
        backs.append(over(result, both_ways))
        return mark

    def own(js, *after):
        packed = (tuple(far[j] for j in js), tuple(near[j] for j in js))
        result, mark = project(js, spots, pairs, ours, OURS, wide, packed, jnp.float32, after)
        owns.append(result)
        return mark

    def attention(at, js, *after):
        left, right, mark = attend_chunks(
            js, owns[at], [backs[j] for j in js], cosine, sine, reach, held, after
        )
        contexts.append((left, over(right, swap)))
        return mark

    for at in range(2):
        made, mark = relay(onward, came[1 - at], first[1 - at], (mark,))
        came.append(lax.ppermute(made, "replica", along[at]))
    mark = stage(1, mark)
    mark = product(0, mark)
    mark = own((0,), mark)
    mark = stage(2, mark)
    mark = product(1, mark)
    mark = own((1,), mark)
    made, mark = unpack(backs[0], depth, (mark, far[2]))
    near.append(made)
    far.append(over(made, across))
    mark = product(2, mark)
    *held, mark = keep_keys(spots, owns[0], backs[0], cosine, sine, (mark,))
    mark = product(3, mark, backs[1])
    parts = tuple(tuple(rows_of[j] for j in (2, 3)) for rows_of in (far, near))
    left, right, made, mark = attend_and_project(
        ((1,), owns[1], [backs[1]], cosine, sine, reach, held),
        ((2, 3), spots, pairs, ours, OURS, wide, parts),
        (mark,),
    )
    contexts.append((left, over(right, swap)))
    owns.append(made)
    mark = attention(2, (2, 3), mark)
    new_params, new_momentum, mark = outer_update(table, values, came, (mark,))

    mine = jnp.concatenate([first for first, _ in contexts], 1)
    came = jnp.concatenate([second for _, second in contexts], 1)
    context = jnp.where(
        core == 0, jnp.concatenate([mine, came], 1), jnp.concatenate([came, mine], 1)
    )
    return (context[None], new_params[None], new_momentum[None])


def step(exchange, tokens, positions, weights, anchor, momentum):
    context = attention_step(tokens, positions, weights)
    new_params, new_momentum = outer_step(exchange, weights, anchor, momentum)
    return (context, new_params, new_momentum)


def body(tokens, positions, partner, weights, anchor, momentum):
    count = lax.axis_size("replica")
    arrays = (tokens, positions, weights, anchor, momentum)
    if count == SQUARE and lax.axis_size("fsdp") == LINE * CORES:
        return line_step(partner, *arrays)
    return step(lambda values: exchange_any(values, partner, count), *arrays)


def solution(mesh):
    placed = (
        P("replica", "fsdp", None),
        P("replica", "fsdp"),
        P(),
        P("replica", "fsdp", None),
        P("replica", "fsdp", None),
        P("replica", "fsdp", None),
    )
    return jax.shard_map(
        body,
        mesh=mesh,
        in_specs=placed,
        out_specs=(
            P("replica", "fsdp", None),
            P("replica", "fsdp", None),
            P("replica", "fsdp", None),
        ),
        check_vma=False,
    )
```
